32 devices in a mesh: section: 4 (over y, x), mp: 2 (over core), dp: 4 (over z).
Axes of the slice: x: 2, y: 2, z: 4, core: 2. Of those that a mesh axis runs over, the one named last changes fastest.
Arguments:
- tokens: bfloat16 [512, 4096], P(('dp', 'section', 'mp')), parts along dimension 0, may hold values from -6 to 6
- mix_gain: bfloat16 [4096], replicated, may hold values from 0.099609375 to 1.8984375
- inner_weight: bfloat16 [4096, 2048], P(None, ('section', 'mp')), may hold values from -0.09375 to 0.09375
- gate_weight: bfloat16 [4096, 2048], P(None, ('section', 'mp')), may hold values from -0.09375 to 0.09375
- group_weight: bfloat16 [4096, 1024], P(None, ('section', 'mp')), may hold values from -0.09375 to 0.09375
- step_weight: bfloat16 [4096, 32], P(None, ('section', 'mp')), may hold values from -0.09375 to 0.09375
- step_bias: float32 [32], P(('section', 'mp')), may hold values from -4 to -1
- rate_log: float32 [32], P(('section', 'mp')), may hold values from -3 to 1
- skip_scale: float32 [32], P(('section', 'mp')), may hold values from 0.5 to 1.5
- norm_gain: bfloat16 [2048], P(('section', 'mp')), may hold values from 0.099609375 to 1.8984375
- out_weight: bfloat16 [2048, 4096], P(('section', 'mp')), may hold values from -0.125 to 0.125
- earlier_states: float32 [16, 2, 4, 4, 64, 256], P(('dp', 'section'), 'mp'), parts along dimension 0, may hold values from -0.8 to 0.8
- earlier_decay: float32 [16, 2, 4, 4], P(('dp', 'section'), 'mp'), parts along dimension 0, may hold values from -2 to -0.01
- attention_gain: bfloat16 [4096], replicated, may hold values from 0.099609375 to 1.8984375
- query_weight: bfloat16 [4096, 1024], P(None, ('section', 'mp')), may hold values from -1 to 1
- keyval_weight: bfloat16 [4096, 512], P(None, ('section', 'mp')), may hold values from -1 to 1
- context_weight: bfloat16 [1024, 4096], P(('section', 'mp')), may hold values from -0.1875 to 0.1875
- key_cache: bfloat16 [32768, 2, 256], P(('dp', 'section'), 'mp'), parts along dimension 0, may hold values from -6 to 6
- doc_offset: int32 [4], P('dp'), parts along dimension 0, may hold values from 1 to 8192
Outputs:
- hidden_out: bfloat16 [512, 4096], P(('dp', 'section', 'mp')), parts along dimension 0
- final_state: float32 [128, 64, 256], P(('dp', 'section', 'mp')), parts along dimension 0
- window_kv: bfloat16 [512, 2, 256], P('dp', 'mp'), parts along dimension 0
The draws below stay inside these ranges and needn't reach their ends.
There are 4 independent parts, one for each index of `dp`. The reference program is written for one: setup_inputs(seed, part) draws one part's arguments, and reference() takes and returns one part's arrays. A program takes and returns all parts, laid end to end along the dimension named above; an argument that names none is the same for every part. Nothing has to cross between parts.
Inputs may be any that keep to these rules, and one draw needn't show every extreme that they name: Cache positions below 8192 minus doc_offset belong to earlier documents.
All inputs are finite; a program needn't handle non-finite values.
Results may differ from the reference program's by a relative error of at most 0.033.
Values may be sent and summed in bfloat16 or wider, within the bound.
A program may use at most 128 MiB of HBM per device.

```python
import math
import jax
import jax.numpy as jnp
from jax import lax

D = 4096
MH_DEV = 4
HP = 64
NS = 256
HD = 128
HM = 32
QH = 8
WIN = 128
CACHE = 8192
PREV = 4
N_SECTION = 4
N_MP = 2


def draw_query_weight(key, part):
    noise_key = jax.random.fold_in(key, 5)
    entries = jnp.clip(jax.random.normal(noise_key, (D, QH, HD), jnp.float32), -6.0, 6.0) / math.sqrt(D)
    return jnp.clip(entries.reshape(D, QH * HD), -1.0, 1.0).astype(jnp.bfloat16)


def draw_keyval_weight(key, part):
    noise_key = jax.random.fold_in(key, 6)
    entries = jnp.clip(jax.random.normal(noise_key, (D, N_MP, 2 * HD), jnp.float32), -6.0, 6.0) / math.sqrt(D)
    quarter = 2 * HD // N_SECTION
    ordered = jnp.transpose(entries.reshape(D, N_MP, N_SECTION, quarter), (0, 2, 1, 3)).reshape(D, 2 * HD * N_MP)
    return jnp.clip(ordered, -1.0, 1.0).astype(jnp.bfloat16)


def levels(own_key, dims, cuts, smallest, top_value):
    level = 1.0
    for dim, parts in cuts:
        heights = jax.random.uniform(jax.random.fold_in(jax.random.fold_in(own_key, 6), dim), (parts,), jnp.float32, smallest / len(cuts), top_value / len(cuts))
        level = level * jnp.repeat(jnp.exp(heights), dims[dim] // parts).reshape((-1,) + (1,) * (len(dims) - 1 - dim))
    return level


def bell_draw(key, shape, deviation, bound, cuts=(), kind=jnp.bfloat16):
    drawn = deviation * jax.random.normal(key, shape, jnp.float32)
    if cuts:
        drawn = drawn * levels(key, shape, cuts, -0.22, 0.18)
    return jnp.clip(drawn, -bound, bound).astype(kind)


def setup_inputs(seed: int = 0, part: int = 0) -> dict:
    key_list = jax.random.split(jax.random.key(seed), 20)
    part_keys = jax.random.split(jax.random.fold_in(key_list[19], part), 20)
    tokens = bell_draw(part_keys[0], (WIN, D), 1.0, 6.0, ((0, 8),))
    mix_gain = jnp.clip(1.0 + 0.18 * jax.random.normal(key_list[1], (D,), jnp.float32), 0.099609375, 1.8984375).astype(jnp.bfloat16)
    inner_weight = bell_draw(key_list[2], (D, HM * HP), D ** -0.5, 0.09375, ((1, 8),))
    gate_weight = bell_draw(key_list[3], (D, HM * HP), D ** -0.5, 0.09375, ((1, 8),))
    group_weight = bell_draw(key_list[4], (D, 2 * NS * N_MP), D ** -0.5, 0.09375, ((1, 8),))
    step_weight = bell_draw(key_list[5], (D, HM), D ** -0.5, 0.09375, ((1, 8),))
    step_bias = jnp.clip(-4.0 + 3.0 * jax.random.uniform(key_list[6], (HM,), jnp.float32) ** levels(key_list[6], (HM,), ((0, 8),), -0.2, 0.2), -4.0, -1.0)
    rate_log = jnp.clip(-3.0 + 4.0 * jax.random.uniform(key_list[7], (HM,), jnp.float32) ** levels(key_list[7], (HM,), ((0, 8),), -0.2, 0.2), -3.0, 1.0)
    skip_scale = jnp.clip(0.5 + 1.0 * jax.random.uniform(key_list[8], (HM,), jnp.float32) ** levels(key_list[8], (HM,), ((0, 8),), -0.2, 0.2), 0.5, 1.5)
    norm_gain = jnp.clip(1.0 + 0.18 * jax.random.normal(key_list[9], (HM * HP,), jnp.float32), 0.099609375, 1.8984375).astype(jnp.bfloat16)
    out_weight = bell_draw(key_list[10], (HM * HP, D), (HM * HP) ** -0.5, 0.125, ((0, 8),))
    earlier_states = bell_draw(part_keys[11], (PREV, N_MP, N_SECTION, MH_DEV, HP, NS), 0.1, 0.8, ((0, 4), (1, 2)), jnp.float32)
    earlier_decay = jnp.clip(-2.0 + 1.99 * jax.random.uniform(part_keys[12], (PREV, N_MP, N_SECTION, MH_DEV), jnp.float32) ** levels(part_keys[12], (PREV, N_MP, N_SECTION, MH_DEV), ((0, 4), (1, 2)), -0.2, 0.2), -2.0, -0.01)
    attention_gain = jnp.clip(1.0 + 0.18 * jax.random.normal(key_list[13], (D,), jnp.float32), 0.099609375, 1.8984375).astype(jnp.bfloat16)
    query_weight = draw_query_weight(jax.random.fold_in(key_list[19], 71), part)
    keyval_weight = draw_keyval_weight(jax.random.fold_in(key_list[19], 71), part)
    context_weight = bell_draw(key_list[16], (QH * HD, D), (QH * HD) ** -0.5, 0.1875, ((0, 8),))
    key_cache = bell_draw(part_keys[17], (CACHE, N_MP, 2 * HD), 1.0, 6.0, ((0, 4), (1, 2)))
    doc_offset = jax.random.randint(part_keys[18], (1,), 1, CACHE + 1).astype(jnp.int32)
    return {"tokens": tokens, "mix_gain": mix_gain, "inner_weight": inner_weight, "gate_weight": gate_weight, "group_weight": group_weight, "step_weight": step_weight, "step_bias": step_bias, "rate_log": rate_log, "skip_scale": skip_scale, "norm_gain": norm_gain, "out_weight": out_weight, "earlier_states": earlier_states, "earlier_decay": earlier_decay, "attention_gain": attention_gain, "query_weight": query_weight, "keyval_weight": keyval_weight, "context_weight": context_weight, "key_cache": key_cache, "doc_offset": doc_offset}


epsilon = 1e-05
precise = lax.Precision.HIGHEST
masked_low = -1e+30

def rms_rows(values, gain):
    widened = values.astype(jnp.float32)
    inverse = lax.rsqrt(lax.optimization_barrier(jnp.mean(widened * widened, axis=-1, keepdims=True)) + epsilon)
    return (widened * inverse * gain.astype(jnp.float32)).astype(jnp.bfloat16)

def group_columns(projected, width):
    row_count = projected.shape[0]
    pieces = projected.reshape(row_count, N_SECTION, N_MP, width // N_SECTION)
    return jnp.transpose(pieces, (0, 2, 1, 3)).reshape(row_count, N_MP, width)

def device_sum(rows, weight, blocks):
    row_count = rows.shape[0]
    width = rows.shape[1] // blocks
    row_blocks = jnp.transpose(rows.reshape(row_count, blocks, width), (1, 0, 2))
    weight_blocks = weight.reshape(blocks, width, weight.shape[1])

    def add_block(total, pieces):
        term = jnp.dot(pieces[0], pieces[1], preferred_element_type=jnp.float32).astype(jnp.bfloat16)
        term = lax.optimization_barrier(term)
        return (total + term.astype(jnp.float32), None)
    total, _ = lax.scan(add_block, jnp.zeros((row_count, weight.shape[1]), jnp.float32), (row_blocks, weight_blocks))
    return total

def reference(tokens, mix_gain, inner_weight, gate_weight, group_weight, step_weight, step_bias, rate_log, skip_scale, norm_gain, out_weight, earlier_states, earlier_decay, attention_gain, query_weight, keyval_weight, context_weight, key_cache, doc_offset):
    mamba_heads = MH_DEV * N_SECTION * N_MP
    query_heads = N_SECTION * N_MP
    normed = rms_rows(tokens, mix_gain)
    inner = jnp.dot(normed, inner_weight, preferred_element_type=jnp.float32).astype(jnp.bfloat16)
    gates = jnp.dot(normed, gate_weight, preferred_element_type=jnp.float32)
    grouped = group_columns(jnp.dot(normed, group_weight, preferred_element_type=jnp.float32).astype(jnp.bfloat16), 2 * NS)
    steps_all = jax.nn.softplus(jnp.dot(normed, step_weight, preferred_element_type=jnp.float32) + step_bias)
    rates = -jnp.exp(rate_log)
    states_all = jnp.transpose(earlier_states, (0, 2, 1, 3, 4, 5)).reshape(PREV, mamba_heads, HP, NS)
    decays_all = jnp.transpose(earlier_decay, (0, 2, 1, 3)).reshape(PREV, mamba_heads)

    def carry_block(state, pieces):
        return (jnp.exp(pieces[1])[:, None, None] * state + pieces[0], None)
    start_state, _ = lax.scan(carry_block, jnp.zeros((mamba_heads, HP, NS), jnp.float32), (states_all, decays_all))
    position = jnp.arange(WIN, dtype=jnp.int32)
    causal = position[:, None] >= position[None, :]

    def mamba_head(head_index):
        group = head_index // MH_DEV % N_MP
        paired = lax.dynamic_index_in_dim(grouped, group, 1, keepdims=False)
        writer = paired[:, :NS]
        reader = paired[:, NS:]
        inputs_head = lax.dynamic_slice_in_dim(inner, head_index * HP, HP, 1)
        step_sizes = lax.dynamic_index_in_dim(steps_all, head_index, 1, keepdims=False)
        log_decay = jnp.cumsum(step_sizes * rates[head_index])
        affinity = jnp.dot(reader, writer.T, preferred_element_type=jnp.float32)
        spread = log_decay[:, None] - log_decay[None, :]
        mixing = jnp.where(causal, affinity * jnp.exp(jnp.where(causal, spread, 0.0)) * step_sizes[None, :], 0.0).astype(jnp.bfloat16)
        intra = jnp.dot(mixing, inputs_head, preferred_element_type=jnp.float32)
        state_head = start_state[head_index]
        carried = jnp.dot(reader.astype(jnp.float32), state_head.T, precision=precise) * jnp.exp(log_decay)[:, None]
        widened = inputs_head.astype(jnp.float32)
        output_head = intra + carried + skip_scale[head_index] * widened
        tail_weights = jnp.exp(log_decay[-1] - log_decay) * step_sizes
        final_head = jnp.exp(log_decay[-1]) * state_head + jnp.dot((widened * tail_weights[:, None]).T, writer.astype(jnp.float32), precision=precise)
        return (output_head, final_head)
    outputs_heads, final_state = lax.map(mamba_head, jnp.arange(mamba_heads, dtype=jnp.int32))
    mamba_rows = jnp.transpose(outputs_heads, (1, 0, 2))
    gated = mamba_rows * jax.nn.silu(gates.reshape(WIN, mamba_heads, HP))
    head_squares = lax.optimization_barrier(jnp.sum(gated * gated, axis=2)).reshape(WIN, N_SECTION, N_MP, MH_DEV)
    group_squares = lax.optimization_barrier(jnp.sum(lax.optimization_barrier(jnp.sum(head_squares, axis=3)), axis=1))
    spread_back = jnp.broadcast_to(group_squares[:, None, :, None], (WIN, N_SECTION, N_MP, MH_DEV)).reshape(WIN, mamba_heads)
    inverse = lax.rsqrt(spread_back / (N_SECTION * MH_DEV * HP) + epsilon)
    normed_heads = (gated * inverse[:, :, None] * norm_gain.astype(jnp.float32).reshape(mamba_heads, HP)).astype(jnp.bfloat16).reshape(WIN, mamba_heads * HP)
    residual = (tokens.astype(jnp.float32) + device_sum(normed_heads, out_weight, N_SECTION * N_MP)).astype(jnp.bfloat16)
    normed_two = rms_rows(residual, attention_gain)
    queries = jnp.dot(normed_two, query_weight, preferred_element_type=jnp.float32).astype(jnp.bfloat16)
    keyvals = group_columns(jnp.dot(normed_two, keyval_weight, preferred_element_type=jnp.float32).astype(jnp.bfloat16), 2 * HD)
    cache_position = jnp.arange(CACHE, dtype=jnp.int32)
    cache_live = cache_position >= CACHE - doc_offset[0]
    live_all = jnp.concatenate([jnp.broadcast_to(cache_live[None, :], (WIN, CACHE)), causal], axis=1)
    scale = 1.0 / math.sqrt(HD)

    def attention_head(head_index):
        group = head_index % N_MP
        query_head = lax.dynamic_slice_in_dim(queries, head_index * HD, HD, 1)
        cached = lax.dynamic_index_in_dim(key_cache, group, 1, keepdims=False)
        fresh = lax.dynamic_index_in_dim(keyvals, group, 1, keepdims=False)
        every = jnp.concatenate([cached, fresh], axis=0)
        logits = jnp.dot(query_head, every[:, :HD].T, preferred_element_type=jnp.float32) * scale
        highest = lax.optimization_barrier(jnp.max(jnp.where(live_all, logits, masked_low), axis=1, keepdims=True))
        weights = jnp.where(live_all, jnp.exp(logits - highest), 0.0)
        totals = lax.optimization_barrier(jnp.sum(weights, axis=1, keepdims=True))
        return (jnp.dot(weights.astype(jnp.bfloat16), every[:, HD:], preferred_element_type=jnp.float32) / totals).astype(jnp.bfloat16)
    contexts = lax.map(attention_head, jnp.arange(query_heads, dtype=jnp.int32))
    context_rows = jnp.transpose(contexts, (1, 0, 2)).reshape(WIN, query_heads * HD)
    hidden_out = (residual.astype(jnp.float32) + device_sum(context_rows, context_weight, query_heads)).astype(jnp.bfloat16)
    return (hidden_out, final_state, keyvals)
```

```python
import functools
import math

import jax
import jax.numpy as jnp
from jax import lax
from jax.experimental import pallas as pl
from jax.experimental.pallas import tpu as pltpu
from jax.sharding import PartitionSpec as P

epsilon = 1e-05
masked_low = -1e30
MESH = pl.DeviceIdType.MESH
f32 = jnp.float32
bf16 = jnp.bfloat16
CHUNKS = 4


def dot(a, b, ca, cb, **kw):
    return lax.dot_general(a, b, (((ca,), (cb,)), ((), ())), preferred_element_type=f32, **kw)


def kernel(
    S, MP,
    tokens, mix_gain, inner_w, gate_w, group_w, step_w, step_bias, rate_log, skip_scale, norm_gain,
    out_w, states, decay, att_gain, query_w, keyval_w, context_w, cache, doc_offset,
    hidden, final_state, window_kv,
    W1, WS, Wo, W2, WKV, Wc, CK, SF, load_sem,
    G1, G2, g1s, g1r, g2s, g2r,
    acc, GP, gps, gpr, STS, ST, sts, str_, DB, dbs, dbr, SQ, sqs, sqr,
    SND1, RCV1, r1s, r1r, MID1, RCM1, m1s, m1r,
    SND2, RCV2, r2s, r2r, MID2, RCM2, m2s, m2r,
    RES, QB, qbs, qbr, KVB, kvs, kvr, ACS, ACR, acs, acr, LS, LR, lss, lsr,
):
    me = lax.axis_index("section")
    mm = lax.axis_index("mp")
    rows, D = tokens.shape
    T = rows * S * MP
    KC = D // CHUNKS
    IW = inner_w.shape[1]
    GW = group_w.shape[1]
    heads = step_w.shape[1]
    HP = IW // heads
    HD = query_w.shape[1]
    KW = keyval_w.shape[1]
    sent = []

    def sec(i):
        return lax.rem(me + i + S, S)

    def core(j):
        return lax.rem(mm + j + MP, MP)

    def rcopy(src, dst, ss, rs, **where):
        return pltpu.make_async_remote_copy(
            src_ref=src, dst_ref=dst, send_sem=ss, recv_sem=rs, device_id=where, device_id_type=MESH
        )

    def send(src, dst, ss, rs, **where):
        d = rcopy(src, dst, ss, rs, **where)
        d.start()
        sent.append(d)

    def arrive(dst, ss, rs, **where):
        rcopy(dst, dst, ss, rs, **where).wait_recv()

    loads = [
        (inner_w, W1.at[:, 0:IW]),
        (gate_w, W1.at[:, IW : 2 * IW]),
        (group_w, W1.at[:, 2 * IW : 2 * IW + GW]),
        (step_w, WS),
        (states.at[0, 0], SF),
        (out_w, Wo),
        (query_w, W2.at[:, 0:HD]),
        (keyval_w, WKV),
        (cache, CK),
        (context_w, Wc),
    ]
    copies = [pltpu.make_async_copy(a, b, load_sem.at[k]) for k, (a, b) in enumerate(loads)]
    for c in copies:
        c.start()

    barrier = pltpu.get_barrier_semaphore()
    for i in range(1, S):
        pl.semaphore_signal(barrier, inc=1, device_id={"section": sec(i)}, device_id_type=MESH)
    for j in range(1, MP):
        pl.semaphore_signal(barrier, inc=1, device_id={"mp": core(j)}, device_id_type=MESH)

    def norm_into(G, values, gain):
        inverse = lax.rsqrt(jnp.mean(values * values, axis=-1, keepdims=True) + epsilon)
        n = (values * inverse * gain).astype(bf16)
        for c in range(CHUNKS):
            G[c, me, mm] = n[:, c * KC : (c + 1) * KC]

    def gather_start(G, ss, rs):
        for c in range(CHUNKS):
            own = G.at[c, me, mm]
            for i in range(1, S):
                send(own, own, ss.at[c, i - 1], rs.at[c, i - 1], section=sec(i))
            for j in range(1, MP):
                k = S - 1 + (j - 1) * S
                send(own, own, ss.at[c, k], rs.at[c, k], mp=core(j))

    def gather_chunk(G, ss, rs, c):
        for i in range(1, S):
            got = G.at[c, sec(-i), mm]
            arrive(got, ss.at[c, i - 1], rs.at[c, i - 1], section=sec(i))
            for j in range(1, MP):
                k = S - 1 + (j - 1) * S + i
                send(got, got, ss.at[c, k], rs.at[c, k], mp=core(j))
        for j in range(1, MP):
            for i in range(S):
                k = S - 1 + (j - 1) * S + i
                got = G.at[c, sec(-i), core(-j)]
                arrive(got, ss.at[c, k], rs.at[c, k], mp=core(j))

    norm_into(G1, tokens[...].astype(f32), mix_gain[...].astype(f32))
    DB[me] = jnp.zeros(DB.shape[1:], f32)
    DB[me, 0:S, 0:heads] = decay[0, 0]
    pl.semaphore_wait(barrier, S - 1 + MP - 1)
    gather_start(G1, g1s, g1r)

    copies[4].wait()
    for q in range(S):
        STS[q] = SF[q].reshape(IW, SF.shape[-1]).astype(bf16)
    ST[me] = STS[me]
    for i in range(1, S):
        send(DB.at[me], DB.at[me], dbs.at[i - 1], dbr.at[i - 1], section=sec(i))
        send(STS.at[sec(i)], ST.at[me], sts.at[i - 1], str_.at[i - 1], section=sec(i))

    copies[3].wait()
    W1[:, 2 * IW + GW :] = jnp.zeros((D, W1.shape[1] - 2 * IW - GW), bf16)
    W1[:, 2 * IW + GW : 2 * IW + GW + heads] = WS[...]
    copies[7].wait()
    W2[:, HD:] = jnp.zeros((D, W2.shape[1] - HD), bf16)
    W2[:, HD : HD + KW] = WKV[...]
    for k in (0, 1, 2):
        copies[k].wait()

    def project(G, ss, rs, W):
        total = None
        for c in range(CHUNKS):
            gather_chunk(G, ss, rs, c)
            part = jnp.dot(
                G[c].reshape(T, KC), W[c * KC : (c + 1) * KC, :], preferred_element_type=f32
            )
            if c == 0:
                acc[:, 0 : W.shape[1]] = part
            else:
                acc[:, 0 : W.shape[1]] += part

    project(G1, g1s, g1r, W1)
    GP[me] = acc[:, 2 * IW : 2 * IW + GW].astype(bf16)
    for i in range(1, S):
        send(GP.at[me], GP.at[me], gps.at[i - 1], gpr.at[i - 1], section=sec(i))

    lane = lax.broadcasted_iota(jnp.int32, (1, 128), 1)
    wide = lax.broadcasted_iota(jnp.int32, (1, IW), 1) // HP

    def spread_scalars(ref, index):
        row = jnp.zeros(index.shape, f32)
        for h in range(heads):
            row = jnp.where(index == h, ref[h], row)
        return row

    def expand(cols):
        full = jnp.broadcast_to(cols[:, 0:1], (cols.shape[0], IW))
        for h in range(1, heads):
            full = jnp.where(wide == h, cols[:, h : h + 1], full)
        return full

    x = acc[:, 2 * IW + GW : 2 * IW + GW + 128] + spread_scalars(step_bias, lane)
    step = jnp.maximum(x, 0.0) + jnp.log1p(jnp.exp(-jnp.abs(x)))
    rates = -jnp.exp(spread_scalars(rate_log, lane))
    t_row = lax.broadcasted_iota(jnp.int32, (T, T), 0)
    t_col = lax.broadcasted_iota(jnp.int32, (T, T), 1)
    causal = t_row >= t_col
    log_decay = jnp.dot(
        causal.astype(f32), step * rates, preferred_element_type=f32, precision=lax.Precision.HIGHEST
    )
    ld_rows = log_decay.T
    st_rows = step.T
    inner = acc[:, 0:IW].astype(bf16)
    inner_f = inner.astype(f32)
    gates = acc[:, IW : 2 * IW]
    silu = gates / (1.0 + jnp.exp(-gates))
    skip = spread_scalars(skip_scale, wide) * inner_f
    reach = expand(jnp.exp(log_decay))

    for i in range(1, S):
        arrive(DB.at[sec(-i)], dbs.at[i - 1], dbr.at[i - 1], section=sec(i))
        arrive(ST.at[sec(-i)], sts.at[i - 1], str_.at[i - 1], section=sec(i))
    later = jnp.zeros((1, 128), f32)
    factors = [None] * S
    for c in reversed(range(S)):
        factors[c] = jnp.exp(later)
        later = later + DB[c, pl.ds(me, 1), :]
    for h in range(heads):
        total = factors[0][:, h : h + 1] * ST[0, h * HP : (h + 1) * HP, :].astype(f32)
        for c in range(1, S):
            total += factors[c][:, h : h + 1] * ST[c, h * HP : (h + 1) * HP, :].astype(f32)
        final_state[h] = total
    start = jnp.concatenate([final_state[h].astype(bf16) for h in range(heads)], axis=0)

    for i in range(1, S):
        arrive(GP.at[sec(-i)], gps.at[i - 1], gpr.at[i - 1], section=sec(i))
    writer = jnp.concatenate([GP[s] for s in range(S // 2)], axis=1)
    reader = jnp.concatenate([GP[s] for s in range(S // 2, S)], axis=1)
    affinity = dot(reader, writer, 1, 1)
    y = dot(reader, start, 1, 1) * reach + skip
    intra = jnp.zeros((T, IW), f32)
    for h in range(heads):
        gap = jnp.where(causal, log_decay[:, h : h + 1] - ld_rows[h : h + 1, :], 0.0)
        mixing = jnp.where(causal, affinity * jnp.exp(gap) * st_rows[h : h + 1, :], 0.0).astype(bf16)
        intra = jnp.where(wide == h, jnp.dot(mixing, inner, preferred_element_type=f32), intra)
    gated = (y + intra) * silu
    SQ[me] = dot(jnp.ones((8, IW), f32), gated * gated, 1, 1, precision=lax.Precision.HIGHEST)
    for i in range(1, S):
        send(SQ.at[me], SQ.at[me], sqs.at[i - 1], sqr.at[i - 1], section=sec(i))
    lhs = (gated * norm_gain[...].astype(f32)).astype(bf16)

    def reduce_send(SND, ss, rs, c, value):
        value = value.astype(bf16).reshape(S, MP, rows, KC)
        for s in range(S):
            for m in range(MP):
                SND[c, m, s] = value[s, m]

    def scatter_pairs(SND, RCV, ss, rs, c):
        for j in range(1, MP):
            send(SND.at[c, core(j)], RCV.at[c, j - 1], ss.at[c, j - 1], rs.at[c, j - 1], mp=core(j))

    def scatter_sections(SND, RCV, ss, rs, MID, RCM, ms, mr, c):
        for j in range(1, MP):
            arrive(RCV.at[c, j - 1], ss.at[c, j - 1], rs.at[c, j - 1], mp=core(j))
        total = SND[c, mm].astype(f32)
        for j in range(1, MP):
            total += RCV[c, j - 1].astype(f32)
        MID[c] = total.astype(bf16)
        for i in range(1, S):
            send(MID.at[c, sec(i)], RCM.at[c, i - 1], ms.at[c, i - 1], mr.at[c, i - 1], section=sec(i))

    def scatter_end(MID, RCM, ms, mr, c):
        total = MID[c, me].astype(f32)
        for i in range(1, S):
            arrive(RCM.at[c, i - 1], ms.at[c, i - 1], mr.at[c, i - 1], section=sec(i))
            total += RCM[c, i - 1].astype(f32)
        return total

    copies[5].wait()
    inverse = None
    for c in range(CHUNKS):
        value = jnp.dot(lhs, Wo[:, c * KC : (c + 1) * KC], preferred_element_type=f32)
        if inverse is None:
            squares = SQ[me]
            for i in range(1, S):
                arrive(SQ.at[sec(-i)], sqs.at[i - 1], sqr.at[i - 1], section=sec(i))
                squares += SQ[sec(-i)]
            inverse = lax.rsqrt(squares / (S * IW) + epsilon)
            inverse = jnp.broadcast_to(inverse[0:1, :], (128, T)).T[:, 0:1]
        reduce_send(SND1, r1s, r1r, c, value * inverse)
        scatter_pairs(SND1, RCV1, r1s, r1r, c)
        if c:
            scatter_sections(SND1, RCV1, r1s, r1r, MID1, RCM1, m1s, m1r, c - 1)
    scatter_sections(SND1, RCV1, r1s, r1r, MID1, RCM1, m1s, m1r, CHUNKS - 1)

    tail = jnp.exp(log_decay[T - 1 : T, :] - log_decay) * step
    added = dot((inner_f * expand(tail)).astype(bf16), writer, 0, 0)
    last = jnp.exp(log_decay[T - 1 : T, :])
    for h in range(heads):
        final_state[h] = last[:, h : h + 1] * final_state[h] + added[h * HP : (h + 1) * HP, :]

    for c in range(CHUNKS):
        cols = slice(c * KC, (c + 1) * KC)
        RES[:, cols] = (
            tokens[:, cols].astype(f32) + scatter_end(MID1, RCM1, m1s, m1r, c)
        ).astype(bf16)
    norm_into(G2, RES[...].astype(f32), att_gain[...].astype(f32))
    gather_start(G2, g2s, g2r)
    copies[6].wait()
    copies[8].wait()
    project(G2, g2s, g2r, W2)
    QB[me] = acc[:, 0:HD].astype(bf16)
    for i in range(1, S):
        send(QB.at[me], QB.at[me], qbs.at[i - 1], qbr.at[i - 1], section=sec(i))
    KVB[me] = acc[:, HD : 2 * HD].astype(bf16)
    for i in range(1, S):
        send(KVB.at[me], KVB.at[me], kvs.at[i - 1], kvr.at[i - 1], section=sec(i))

    scale = 1.0 / math.sqrt(HD)
    held = CK.shape[0]
    position = lax.broadcasted_iota(jnp.int32, (held, 1), 0) + me * held
    bias = jnp.where(position >= held * S - doc_offset[0], 0.0, masked_low).astype(f32)

    def attend(q, keys, values, low):
        logits = dot(keys, q, 1, 1) + low
        top = jnp.max(logits, axis=0, keepdims=True)
        weights = jnp.exp((logits - top) * scale)
        total = jnp.sum(weights, axis=0, keepdims=True)
        out = dot(values, weights.astype(bf16), 0, 0)
        return top * scale, total, out

    def cached(q):
        return attend(q, CK[:, 0:HD], CK[:, HD : 2 * HD], bias)

    for i in range(1, S):
        slot = sec(-i)
        arrive(QB.at[slot], qbs.at[i - 1], qbr.at[i - 1], section=sec(i))
        top, total, out = cached(QB[slot])
        ACS[i - 1] = (out / total).astype(bf16)
        LS[i - 1, 0:8] = jnp.broadcast_to(top, (8, T))
        LS[i - 1, 8:16] = jnp.broadcast_to(total, (8, T))
        send(LS.at[i - 1], LR.at[i - 1], lss.at[i - 1], lsr.at[i - 1], section=slot)
        send(ACS.at[i - 1], ACR.at[i - 1], acs.at[i - 1], acr.at[i - 1], section=slot)
    parts = [cached(QB[me])]
    for i in range(1, S):
        arrive(KVB.at[sec(-i)], kvs.at[i - 1], kvr.at[i - 1], section=sec(i))
    pieces = jnp.concatenate([KVB[s][:, 0:KW].astype(f32) for s in range(S)], axis=1).astype(bf16)
    window_kv[...] = pieces
    new_low = jnp.where(t_row <= t_col, 0.0, masked_low).astype(f32)
    parts.append(attend(QB[me], pieces[:, 0:HD], pieces[:, HD : 2 * HD], new_low))
    copies[9].wait()
    top = jnp.maximum(parts[0][0], parts[1][0])
    for i in range(1, S):
        arrive(LR.at[i - 1], lss.at[i - 1], lsr.at[i - 1], section=sec(i))
        top = jnp.maximum(top, LR[i - 1, 0:1, :])
    total = jnp.zeros((1, T), f32)
    context = jnp.zeros((HD, T), f32)
    for p in parts:
        weight = jnp.exp(p[0] - top)
        total += weight * p[1]
        context += weight * p[2]
    for i in range(1, S):
        weight = jnp.exp(LR[i - 1, 0:1, :] - top) * LR[i - 1, 8:9, :]
        total += weight
        arrive(ACR.at[i - 1], acs.at[i - 1], acr.at[i - 1], section=sec(i))
        context += weight * ACR[i - 1].astype(f32)
    context = (context / total).T.astype(bf16)

    for c in range(CHUNKS):
        value = jnp.dot(context, Wc[:, c * KC : (c + 1) * KC], preferred_element_type=f32)
        reduce_send(SND2, r2s, r2r, c, value)
        scatter_pairs(SND2, RCV2, r2s, r2r, c)
        if c:
            scatter_sections(SND2, RCV2, r2s, r2r, MID2, RCM2, m2s, m2r, c - 1)
    scatter_sections(SND2, RCV2, r2s, r2r, MID2, RCM2, m2s, m2r, CHUNKS - 1)
    for c in range(CHUNKS):
        cols = slice(c * KC, (c + 1) * KC)
        hidden[:, cols] = (
            RES[:, cols].astype(f32) + scatter_end(MID2, RCM2, m2s, m2r, c)
        ).astype(bf16)
    for d in sent:
        d.wait_send()


def local(
    S, MP,
    tokens, mix_gain, inner_w, gate_w, group_w, step_w, step_bias, rate_log, skip_scale, norm_gain,
    out_w, states, decay, att_gain, query_w, keyval_w, context_w, cache, doc_offset,
):
    rows, D = tokens.shape
    T = rows * S * MP
    KC = D // CHUNKS
    IW = inner_w.shape[1]
    GW = group_w.shape[1]
    heads = step_w.shape[1]
    HP = IW // heads
    NS = states.shape[-1]
    HD = query_w.shape[1]
    dma = pltpu.SemaphoreType.DMA
    vmem = pltpu.VMEM

    def both(*shape):
        return [dma(shape), dma(shape)]

    def scatter():
        return [
            vmem((CHUNKS, MP, S, rows, KC), bf16), vmem((CHUNKS, MP - 1, S, rows, KC), bf16),
            *both(CHUNKS, MP - 1),
            vmem((CHUNKS, S, rows, KC), bf16), vmem((CHUNKS, S - 1, rows, KC), bf16),
            *both(CHUNKS, S - 1),
        ]

    hops = S - 1 + (MP - 1) * S
    scratch = [
        vmem((D, 2 * IW + GW + 128), bf16), vmem(step_w.shape, bf16), vmem(out_w.shape, bf16),
        vmem((D, 2 * HD), bf16), vmem(keyval_w.shape, bf16), vmem(context_w.shape, bf16),
        vmem((cache.shape[0], 2 * HD), bf16), vmem(states.shape[2:], f32), dma((10,)),
        vmem((CHUNKS, S, MP, rows, KC), bf16), vmem((CHUNKS, S, MP, rows, KC), bf16),
        *both(CHUNKS, hops), *both(CHUNKS, hops),
        vmem((T, 2 * IW + GW + 128), f32),
        vmem((S, T, GW), bf16), *both(S - 1),
        vmem((S, IW, NS), bf16), vmem((S, IW, NS), bf16), *both(S - 1),
        vmem((S, 8, 128), f32), *both(S - 1),
        vmem((S, 8, T), f32), *both(S - 1),
        *scatter(), *scatter(),
        vmem((rows, D), bf16),
        vmem((S, T, HD), bf16), *both(S - 1),
        vmem((S, T, HD), bf16), *both(S - 1),
        vmem((S - 1, HD, T), bf16), vmem((S - 1, HD, T), bf16), *both(S - 1),
        vmem((S - 1, 16, T), f32), vmem((S - 1, 16, T), f32), *both(S - 1),
    ]
    v = pl.BlockSpec(memory_space=pltpu.VMEM)
    a = pl.BlockSpec(memory_space=pl.ANY)
    s = pl.BlockSpec(memory_space=pltpu.SMEM)
    hidden, final_state, window_kv = pl.pallas_call(
        functools.partial(kernel, S, MP),
        out_shape=(
            jax.ShapeDtypeStruct((rows, D), bf16),
            jax.ShapeDtypeStruct((heads, HP, NS), f32),
            jax.ShapeDtypeStruct((T, 2 * HD), bf16),
        ),
        in_specs=[v, v, a, a, a, a, s, s, s, v, a, a, v, v, a, a, a, a, s],
        out_specs=(v, v, v),
        scratch_shapes=scratch,
        compiler_params=pltpu.CompilerParams(
            collective_id=0, has_side_effects=True, vmem_limit_bytes=60 * 1024 * 1024
        ),
    )(
        tokens, mix_gain.reshape(1, D), inner_w, gate_w, group_w, step_w, step_bias, rate_log,
        skip_scale, norm_gain.reshape(1, IW), out_w, states, decay, att_gain.reshape(1, D),
        query_w, keyval_w, context_w, cache.reshape(cache.shape[0], 2 * HD), doc_offset,
    )
    return hidden, final_state, window_kv[:, None, :]


def solution(mesh):
    S, MP = mesh.shape["section"], mesh.shape["mp"]
    both = ("section", "mp")
    in_specs = (
        P(("dp", "section", "mp"), None),
        P(),
        P(None, both),
        P(None, both),
        P(None, both),
        P(None, both),
        P(both),
        P(both),
        P(both),
        P(both),
        P(both, None),
        P(("dp", "section"), "mp", None, None, None, None),
        P(("dp", "section"), "mp", None, None),
        P(),
        P(None, both),
        P(None, both),
        P(both, None),
        P(("dp", "section"), "mp", None),
        P("dp"),
    )
    out_specs = (
        P(("dp", "section", "mp"), None),
        P(("dp", "section", "mp"), None, None),
        P("dp", "mp", None),
    )
    return jax.shard_map(
        functools.partial(local, S, MP), mesh=mesh, in_specs=in_specs, out_specs=out_specs, check_vma=False
    )
```

```python
import functools
import math

import jax
import jax.numpy as jnp
from jax import lax
from jax.experimental import pallas as pl
from jax.experimental.pallas import tpu as pltpu
from jax.sharding import PartitionSpec as P

epsilon = 1e-05
masked_low = -1e30
MESH = pl.DeviceIdType.MESH
f32 = jnp.float32
bf16 = jnp.bfloat16
CHUNKS = 4


def dot(a, b, ca, cb, **kw):
    return lax.dot_general(a, b, (((ca,), (cb,)), ((), ())), preferred_element_type=f32, **kw)


def kernel(
    S, MP,
    tokens, mix_gain, inner_w, gate_w, group_w, step_w, step_bias, rate_log, skip_scale, norm_gain,
    out_w, states, decay, att_gain, query_w, keyval_w, context_w, cache, doc_offset,
    hidden, final_state, window_kv,
    W1, Wo, W2, WKV, Wc, CK, SF, load_sem,
    G1, G2, g1s, g1r, g2s, g2r,
    acc, GP, gps, gpr, STS, ST, sts, str_, DB, dbs, dbr, SQ, sqs, sqr,
    SND1, RCV1, r1s, r1r, MID1, RCM1, m1s, m1r,
    SND2, RCV2, r2s, r2r, MID2, RCM2, m2s, m2r,
    RES, QB, qbs, qbr, KVB, kvs, kvr, ACS, ACR, acs, acr, LS, LR, lss, lsr,
):
    me = lax.axis_index("section")
    mm = lax.axis_index("mp")
    rows, D = tokens.shape
    T = rows * S * MP
    KC = D // CHUNKS
    IW = inner_w.shape[1]
    GW = group_w.shape[1]
    heads = step_w.shape[0]
    HP = IW // heads
    HD = query_w.shape[1]
    KW = keyval_w.shape[0]
    sent = []

    def sec(i):
        return lax.rem(me + i + S, S)

    def core(j):
        return lax.rem(mm + j + MP, MP)

    def rcopy(src, dst, ss, rs, **where):
        return pltpu.make_async_remote_copy(
            src_ref=src, dst_ref=dst, send_sem=ss, recv_sem=rs, device_id=where, device_id_type=MESH
        )

    def send(src, dst, ss, rs, **where):
        d = rcopy(src, dst, ss, rs, **where)
        d.start()
        sent.append(d)

    def arrive(dst, ss, rs, **where):
        rcopy(dst, dst, ss, rs, **where).wait_recv()

    loads = [
        (inner_w, W1.at[:, 0:IW]),
        (gate_w, W1.at[:, IW : 2 * IW]),
        (group_w, W1.at[:, 2 * IW : 2 * IW + GW]),
        (states.at[0, 0], SF),
        (out_w, Wo),
        (query_w, W2),
        (keyval_w, WKV),
        (cache, CK),
        (context_w, Wc),
    ]
    copies = [pltpu.make_async_copy(a, b, load_sem.at[k]) for k, (a, b) in enumerate(loads)]
    for c in copies:
        c.start()

    barrier = pltpu.get_barrier_semaphore()
    for i in range(1, S):
        pl.semaphore_signal(barrier, inc=1, device_id={"section": sec(i)}, device_id_type=MESH)
    for j in range(1, MP):
        pl.semaphore_signal(barrier, inc=1, device_id={"mp": core(j)}, device_id_type=MESH)

    def norm_into(G, values, gain):
        inverse = lax.rsqrt(jnp.mean(values * values, axis=-1, keepdims=True) + epsilon)
        n = (values * inverse * gain).astype(bf16)
        for c in range(CHUNKS):
            G[c, me, mm] = n[:, c * KC : (c + 1) * KC]

    def gather_start(G, ss, rs):
        for c in range(CHUNKS):
            own = G.at[c, me, mm]
            for i in range(1, S):
                send(own, own, ss.at[c, i - 1], rs.at[c, i - 1], section=sec(i))
            for j in range(1, MP):
                k = S - 1 + (j - 1) * S
                send(own, own, ss.at[c, k], rs.at[c, k], mp=core(j))

    def gather_pass(G, ss, rs, c):
        for i in range(1, S):
            got = G.at[c, sec(-i), mm]
            arrive(got, ss.at[c, i - 1], rs.at[c, i - 1], section=sec(i))
            for j in range(1, MP):
                k = S - 1 + (j - 1) * S + i
                send(got, got, ss.at[c, k], rs.at[c, k], mp=core(j))

    def gather_end(G, ss, rs, c):
        for j in range(1, MP):
            for i in range(S):
                k = S - 1 + (j - 1) * S + i
                got = G.at[c, sec(-i), core(-j)]
                arrive(got, ss.at[c, k], rs.at[c, k], mp=core(j))

    norm_into(G1, tokens[...].astype(f32), mix_gain[...].astype(f32).reshape(1, D))
    DB[me] = jnp.zeros(DB.shape[1:], f32)
    DB[me, 0:S, 0:heads] = decay[0, 0]
    pl.semaphore_wait(barrier, S - 1 + MP - 1)
    gather_start(G1, g1s, g1r)

    copies[3].wait()
    for q in range(S):
        STS[q] = SF[q].reshape(IW, SF.shape[-1]).astype(bf16)
    ST[me] = STS[me]
    for i in range(1, S):
        send(DB.at[me], DB.at[me], dbs.at[i - 1], dbr.at[i - 1], section=sec(i))
        send(STS.at[sec(i)], ST.at[me], sts.at[i - 1], str_.at[i - 1], section=sec(i))

    for k in (0, 1, 2):
        copies[k].wait()

    def project(G, ss, rs, W, side):
        wide, extra = W.shape[1], side.shape[0]
        gather_pass(G, ss, rs, 0)
        for c in range(CHUNKS):
            if c + 1 < CHUNKS:
                gather_pass(G, ss, rs, c + 1)
            gather_end(G, ss, rs, c)
            rowsets = G[c].reshape(T, KC)
            part = jnp.dot(rowsets, W[c * KC : (c + 1) * KC, :], preferred_element_type=f32)
            more = dot(rowsets, side[:, c * KC : (c + 1) * KC], 1, 1)
            if c == 0:
                acc[:, 0:wide] = part
                acc[:, wide : wide + extra] = more
            else:
                acc[:, 0:wide] += part
                acc[:, wide : wide + extra] += more

    acc[:, 2 * IW + GW :] = jnp.zeros((T, 128), f32)
    project(G1, g1s, g1r, W1, step_w)
    GP[me] = acc[:, 2 * IW : 2 * IW + GW].astype(bf16)
    for i in range(1, S):
        send(GP.at[me], GP.at[me], gps.at[i - 1], gpr.at[i - 1], section=sec(i))

    lane = lax.broadcasted_iota(jnp.int32, (1, 128), 1)
    wide = lax.broadcasted_iota(jnp.int32, (1, IW), 1) // HP

    def spread_scalars(ref, index):
        row = jnp.zeros(index.shape, f32)
        for h in range(heads):
            row = jnp.where(index == h, ref[h], row)
        return row

    def expand(cols):
        full = jnp.broadcast_to(cols[:, 0:1], (cols.shape[0], IW))
        for h in range(1, heads):
            full = jnp.where(wide == h, cols[:, h : h + 1], full)
        return full

    x = acc[:, 2 * IW + GW : 2 * IW + GW + 128] + spread_scalars(step_bias, lane)
    step = jnp.maximum(x, 0.0) + jnp.log1p(jnp.exp(-jnp.abs(x)))
    rates = -jnp.exp(spread_scalars(rate_log, lane))
    t_row = lax.broadcasted_iota(jnp.int32, (T, T), 0)
    t_col = lax.broadcasted_iota(jnp.int32, (T, T), 1)
    causal = t_row >= t_col
    log_decay = jnp.dot(
        causal.astype(f32), step * rates, preferred_element_type=f32, precision=lax.Precision.HIGHEST
    )
    ld_rows = log_decay.T
    st_rows = step.T
    inner = acc[:, 0:IW].astype(bf16)
    inner_f = inner.astype(f32)
    gates = acc[:, IW : 2 * IW]
    silu = gates / (1.0 + jnp.exp(-gates))
    skip = spread_scalars(skip_scale, wide) * inner_f
    reach = expand(jnp.exp(log_decay))

    for i in range(1, S):
        arrive(DB.at[sec(-i)], dbs.at[i - 1], dbr.at[i - 1], section=sec(i))
        arrive(ST.at[sec(-i)], sts.at[i - 1], str_.at[i - 1], section=sec(i))
    later = jnp.zeros((1, 128), f32)
    factors = [None] * S
    for c in reversed(range(S)):
        factors[c] = jnp.exp(later)
        later = later + DB[c, pl.ds(me, 1), :]
    for h in range(heads):
        total = factors[0][:, h : h + 1] * ST[0, h * HP : (h + 1) * HP, :].astype(f32)
        for c in range(1, S):
            total += factors[c][:, h : h + 1] * ST[c, h * HP : (h + 1) * HP, :].astype(f32)
        final_state[h] = total
    start = jnp.concatenate([final_state[h].astype(bf16) for h in range(heads)], axis=0)

    for i in range(1, S):
        arrive(GP.at[sec(-i)], gps.at[i - 1], gpr.at[i - 1], section=sec(i))
    writer = jnp.concatenate([GP[s] for s in range(S // 2)], axis=1)
    reader = jnp.concatenate([GP[s] for s in range(S // 2, S)], axis=1)
    affinity = dot(reader, writer, 1, 1)
    y = dot(reader, start, 1, 1) * reach + skip
    intra = jnp.zeros((T, IW), f32)
    for h in range(heads):
        gap = jnp.where(causal, log_decay[:, h : h + 1] - ld_rows[h : h + 1, :], 0.0)
        mixing = jnp.where(causal, affinity * jnp.exp(gap) * st_rows[h : h + 1, :], 0.0).astype(bf16)
        intra = jnp.where(wide == h, jnp.dot(mixing, inner, preferred_element_type=f32), intra)
    gated = (y + intra) * silu
    SQ[me] = dot(jnp.ones((8, IW), f32), gated * gated, 1, 1, precision=lax.Precision.HIGHEST)
    for i in range(1, S):
        send(SQ.at[me], SQ.at[me], sqs.at[i - 1], sqr.at[i - 1], section=sec(i))
    lhs = (gated * norm_gain[...].astype(f32).reshape(1, IW)).astype(bf16)

    def reduce_send(SND, ss, rs, c, value):
        value = value.astype(bf16).reshape(S, MP, rows, KC)
        for s in range(S):
            for m in range(MP):
                SND[c, m, s] = value[s, m]

    def scatter_pairs(SND, RCV, ss, rs, c):
        for j in range(1, MP):
            send(SND.at[c, core(j)], RCV.at[c, j - 1], ss.at[c, j - 1], rs.at[c, j - 1], mp=core(j))

    def scatter_sections(SND, RCV, ss, rs, MID, RCM, ms, mr, c):
        for j in range(1, MP):
            arrive(RCV.at[c, j - 1], ss.at[c, j - 1], rs.at[c, j - 1], mp=core(j))
        total = SND[c, mm].astype(f32)
        for j in range(1, MP):
            total += RCV[c, j - 1].astype(f32)
        MID[c] = total.astype(bf16)
        for i in range(1, S):
            send(MID.at[c, sec(i)], RCM.at[c, i - 1], ms.at[c, i - 1], mr.at[c, i - 1], section=sec(i))

    def scatter_end(MID, RCM, ms, mr, c):
        total = MID[c, me].astype(f32)
        for i in range(1, S):
            arrive(RCM.at[c, i - 1], ms.at[c, i - 1], mr.at[c, i - 1], section=sec(i))
            total += RCM[c, i - 1].astype(f32)
        return total

    copies[4].wait()
    inverse = None
    for c in range(CHUNKS):
        value = jnp.dot(lhs, Wo[:, c * KC : (c + 1) * KC], preferred_element_type=f32)
        if inverse is None:
            squares = SQ[me]
            for i in range(1, S):
                arrive(SQ.at[sec(-i)], sqs.at[i - 1], sqr.at[i - 1], section=sec(i))
                squares += SQ[sec(-i)]
            inverse = lax.rsqrt(squares / (S * IW) + epsilon)
            inverse = jnp.broadcast_to(inverse[0:1, :], (128, T)).T[:, 0:1]
        reduce_send(SND1, r1s, r1r, c, value * inverse)
        scatter_pairs(SND1, RCV1, r1s, r1r, c)
        if c:
            scatter_sections(SND1, RCV1, r1s, r1r, MID1, RCM1, m1s, m1r, c - 1)
    scatter_sections(SND1, RCV1, r1s, r1r, MID1, RCM1, m1s, m1r, CHUNKS - 1)

    tail = jnp.exp(log_decay[T - 1 : T, :] - log_decay) * step
    added = dot((inner_f * expand(tail)).astype(bf16), writer, 0, 0)
    last = jnp.exp(log_decay[T - 1 : T, :])
    for h in range(heads):
        final_state[h] = last[:, h : h + 1] * final_state[h] + added[h * HP : (h + 1) * HP, :]

    for c in range(CHUNKS):
        cols = slice(c * KC, (c + 1) * KC)
        RES[:, cols] = (
            tokens[:, cols].astype(f32) + scatter_end(MID1, RCM1, m1s, m1r, c)
        ).astype(bf16)
    norm_into(G2, RES[...].astype(f32), att_gain[...].astype(f32).reshape(1, D))
    gather_start(G2, g2s, g2r)
    for k in (5, 6, 7):
        copies[k].wait()
    acc[:, HD : 2 * HD] = jnp.zeros((T, HD), f32)
    project(G2, g2s, g2r, W2, WKV)
    QB[me] = acc[:, 0:HD].astype(bf16)
    for i in range(1, S):
        send(QB.at[me], QB.at[me], qbs.at[i - 1], qbr.at[i - 1], section=sec(i))
    KVB[me] = acc[:, HD : 2 * HD].astype(bf16)
    for i in range(1, S):
        send(KVB.at[me], KVB.at[me], kvs.at[i - 1], kvr.at[i - 1], section=sec(i))

    scale = 1.0 / math.sqrt(HD)
    held = CK.shape[0]
    position = lax.broadcasted_iota(jnp.int32, (held, 1), 0) + me * held
    bias = jnp.where(position >= held * S - doc_offset[0], 0.0, masked_low).astype(f32)

    def attend(q, keys, values, low):
        logits = dot(keys, q, 1, 1) + low
        top = jnp.max(logits, axis=0, keepdims=True)
        weights = jnp.exp((logits - top) * scale)
        total = jnp.sum(weights, axis=0, keepdims=True)
        out = dot(values, weights.astype(bf16), 0, 0)
        return top * scale, total, out

    def cached(q):
        return attend(q, CK[:, 0:HD], CK[:, HD : 2 * HD], bias)

    for i in range(1, S):
        slot = sec(-i)
        arrive(QB.at[slot], qbs.at[i - 1], qbr.at[i - 1], section=sec(i))
        top, total, out = cached(QB[slot])
        ACS[i - 1] = (out / total).astype(bf16)
        LS[i - 1, 0:8] = jnp.broadcast_to(top, (8, T))
        LS[i - 1, 8:16] = jnp.broadcast_to(total, (8, T))
        send(LS.at[i - 1], LR.at[i - 1], lss.at[i - 1], lsr.at[i - 1], section=slot)
        send(ACS.at[i - 1], ACR.at[i - 1], acs.at[i - 1], acr.at[i - 1], section=slot)
    parts = [cached(QB[me])]
    for i in range(1, S):
        arrive(KVB.at[sec(-i)], kvs.at[i - 1], kvr.at[i - 1], section=sec(i))
    pieces = jnp.concatenate([KVB[s][:, 0:KW].astype(f32) for s in range(S)], axis=1).astype(bf16)
    window_kv[...] = pieces
    new_low = jnp.where(t_row <= t_col, 0.0, masked_low).astype(f32)
    parts.append(attend(QB[me], pieces[:, 0:HD], pieces[:, HD : 2 * HD], new_low))
    copies[8].wait()
    top = jnp.maximum(parts[0][0], parts[1][0])
    for i in range(1, S):
        arrive(LR.at[i - 1], lss.at[i - 1], lsr.at[i - 1], section=sec(i))
        top = jnp.maximum(top, LR[i - 1, 0:1, :])
    total = jnp.zeros((1, T), f32)
    context = jnp.zeros((HD, T), f32)
    for p in parts:
        weight = jnp.exp(p[0] - top)
        total += weight * p[1]
        context += weight * p[2]
    for i in range(1, S):
        weight = jnp.exp(LR[i - 1, 0:1, :] - top) * LR[i - 1, 8:9, :]
        total += weight
        arrive(ACR.at[i - 1], acs.at[i - 1], acr.at[i - 1], section=sec(i))
        context += weight * ACR[i - 1].astype(f32)
    context = (context / total).T.astype(bf16)

    for c in range(CHUNKS):
        value = jnp.dot(context, Wc[:, c * KC : (c + 1) * KC], preferred_element_type=f32)
        reduce_send(SND2, r2s, r2r, c, value)
        scatter_pairs(SND2, RCV2, r2s, r2r, c)
        if c:
            scatter_sections(SND2, RCV2, r2s, r2r, MID2, RCM2, m2s, m2r, c - 1)
    scatter_sections(SND2, RCV2, r2s, r2r, MID2, RCM2, m2s, m2r, CHUNKS - 1)
    for c in range(CHUNKS):
        cols = slice(c * KC, (c + 1) * KC)
        hidden[:, cols] = (
            RES[:, cols].astype(f32) + scatter_end(MID2, RCM2, m2s, m2r, c)
        ).astype(bf16)
    for d in sent:
        d.wait_send()


def copy_kernel(a, b, c, x, y, z, sem):
    copies = [pltpu.make_async_copy(p, q, sem.at[k]) for k, (p, q) in enumerate(((a, x), (b, y), (c, z)))]
    for d in copies:
        d.start()
    for d in copies:
        d.wait()


def local(
    S, MP,
    tokens, mix_gain, inner_w, gate_w, group_w, step_w, step_bias, rate_log, skip_scale, norm_gain,
    out_w, states, decay, att_gain, query_w, keyval_w, context_w, cache, doc_offset,
):
    rows, D = tokens.shape
    T = rows * S * MP
    KC = D // CHUNKS
    IW = inner_w.shape[1]
    GW = group_w.shape[1]
    heads = step_w.shape[1]
    HP = IW // heads
    NS = states.shape[-1]
    HD = query_w.shape[1]
    dma = pltpu.SemaphoreType.DMA
    vmem = pltpu.VMEM

    def both(*shape):
        return [dma(shape), dma(shape)]

    def scatter():
        return [
            vmem((CHUNKS, MP, S, rows, KC), bf16), vmem((CHUNKS, MP - 1, S, rows, KC), bf16),
            *both(CHUNKS, MP - 1),
            vmem((CHUNKS, S, rows, KC), bf16), vmem((CHUNKS, S - 1, rows, KC), bf16),
            *both(CHUNKS, S - 1),
        ]

    hops = S - 1 + (MP - 1) * S
    scratch = [
        vmem((D, 2 * IW + GW), bf16), vmem(out_w.shape, bf16),
        vmem((D, HD), bf16), vmem(keyval_w.shape[::-1], bf16), vmem(context_w.shape, bf16),
        vmem((cache.shape[0], 2 * HD), bf16), vmem(states.shape[2:], f32), dma((9,)),
        vmem((CHUNKS, S, MP, rows, KC), bf16), vmem((CHUNKS, S, MP, rows, KC), bf16),
        *both(CHUNKS, hops), *both(CHUNKS, hops),
        vmem((T, 2 * IW + GW + 128), f32),
        vmem((S, T, GW), bf16), *both(S - 1),
        vmem((S, IW, NS), bf16), vmem((S, IW, NS), bf16), *both(S - 1),
        vmem((S, 8, 128), f32), *both(S - 1),
        vmem((S, 8, T), f32), *both(S - 1),
        *scatter(), *scatter(),
        vmem((rows, D), bf16),
        vmem((S, T, HD), bf16), *both(S - 1),
        vmem((S, T, HD), bf16), *both(S - 1),
        vmem((S - 1, HD, T), bf16), vmem((S - 1, HD, T), bf16), *both(S - 1),
        vmem((S - 1, 16, T), f32), vmem((S - 1, 16, T), f32), *both(S - 1),
    ]
    v = pl.BlockSpec(memory_space=pltpu.VMEM)
    a = pl.BlockSpec(memory_space=pl.ANY)
    s = pl.BlockSpec(memory_space=pltpu.SMEM)
    hidden, final_state, window_kv = pl.pallas_call(
        functools.partial(kernel, S, MP),
        out_shape=(
            jax.ShapeDtypeStruct((rows, D), bf16),
            jax.ShapeDtypeStruct((heads, HP, NS), f32),
            jax.ShapeDtypeStruct((T, 2 * HD), bf16),
        ),
        in_specs=[v, v, a, a, a, v, s, s, s, v, a, a, v, v, a, a, a, a, s],
        out_specs=(v, v, v),
        scratch_shapes=scratch,
        compiler_params=pltpu.CompilerParams(
            collective_id=0, has_side_effects=True, vmem_limit_bytes=60 * 1024 * 1024
        ),
    )(
        tokens, mix_gain, inner_w, gate_w, group_w, step_w.T, step_bias, rate_log,
        skip_scale, norm_gain, out_w, states, decay, att_gain,
        query_w, keyval_w.T, context_w, cache.reshape(cache.shape[0], 2 * HD), doc_offset,
    )
    results = (hidden, final_state, window_kv)
    hidden, final_state, window_kv = pl.pallas_call(
        copy_kernel,
        out_shape=tuple(jax.ShapeDtypeStruct(x.shape, x.dtype) for x in results),
        in_specs=[a, a, a],
        out_specs=(a, a, a),
        scratch_shapes=[dma((3,))],
    )(*results)
    return hidden, final_state, window_kv[:, None, :]


def solution(mesh):
    S, MP = mesh.shape["section"], mesh.shape["mp"]
    both = ("section", "mp")
    in_specs = (
        P(("dp", "section", "mp"), None),
        P(),
        P(None, both),
        P(None, both),
        P(None, both),
        P(None, both),
        P(both),
        P(both),
        P(both),
        P(both),
        P(both, None),
        P(("dp", "section"), "mp", None, None, None, None),
        P(("dp", "section"), "mp", None, None),
        P(),
        P(None, both),
        P(None, both),
        P(both, None),
        P(("dp", "section"), "mp", None),
        P("dp"),
    )
    out_specs = (
        P(("dp", "section", "mp"), None),
        P(("dp", "section", "mp"), None, None),
        P("dp", "mp", None),
    )
    return jax.shard_map(
        functools.partial(local, S, MP), mesh=mesh, in_specs=in_specs, out_specs=out_specs, check_vma=False
    )
```

```python
import functools
import math

import jax
import jax.numpy as jnp
from jax import lax
from jax.experimental import pallas as pl
from jax.experimental.pallas import tpu as pltpu
from jax.sharding import PartitionSpec as P

epsilon = 1e-05
masked_low = -1e30
MESH = pl.DeviceIdType.MESH
f32 = jnp.float32
bf16 = jnp.bfloat16
CHUNKS = 4


def dot(a, b, ca, cb, **kw):
    return lax.dot_general(a, b, (((ca,), (cb,)), ((), ())), preferred_element_type=f32, **kw)


def kernel(
    S, MP,
    tokens, mix_gain, inner_w, gate_w, group_w, step_w, step_bias, rate_log, skip_scale, norm_gain,
    out_w, states, decay, att_gain, query_w, keyval_w, context_w, cache, doc_offset,
    hidden, final_state, window_kv,
    W1, Wo, W2, WKV, Wc, CK, SF, load_sem,
    G1, G2, g1s, g1r, g2s, g2r,
    acc, GP, gps, gpr, STS, ST, sts, str_, DB, dbs, dbr, SQ, sqs, sqr,
    SND1, RCV1, r1s, r1r, MID1, RCM1, m1s, m1r,
    SND2, RCV2, r2s, r2r, MID2, RCM2, m2s, m2r,
    RES, QB, qbs, qbr, KVB, kvs, kvr, ACS, ACR, acs, acr, LS, LR, lss, lsr,
):
    me = lax.axis_index("section")
    mm = lax.axis_index("mp")
    rows, D = tokens.shape
    T = rows * S * MP
    KC = D // CHUNKS
    IW = inner_w.shape[1]
    GW = group_w.shape[1]
    heads = step_w.shape[0]
    HP = IW // heads
    HD = query_w.shape[1]
    KW = keyval_w.shape[0]
    sent = []

    def sec(i):
        return lax.rem(me + i + S, S)

    def core(j):
        return lax.rem(mm + j + MP, MP)

    def rcopy(src, dst, ss, rs, **where):
        return pltpu.make_async_remote_copy(
            src_ref=src, dst_ref=dst, send_sem=ss, recv_sem=rs, device_id=where, device_id_type=MESH
        )

    def send(src, dst, ss, rs, **where):
        d = rcopy(src, dst, ss, rs, **where)
        d.start()
        sent.append(d)

    def arrive(dst, ss, rs, **where):
        rcopy(dst, dst, ss, rs, **where).wait_recv()

    loads = [
        (inner_w, W1.at[:, 0:IW]),
        (gate_w, W1.at[:, IW : 2 * IW]),
        (group_w, W1.at[:, 2 * IW : 2 * IW + GW]),
        (states.at[0, 0], SF),
        (out_w, Wo),
        (query_w, W2),
        (keyval_w, WKV),
        (cache, CK),
        (context_w, Wc),
    ]
    copies = [pltpu.make_async_copy(a, b, load_sem.at[k]) for k, (a, b) in enumerate(loads)]
    for c in copies:
        c.start()

    barrier = pltpu.get_barrier_semaphore()
    for i in range(1, S):
        pl.semaphore_signal(barrier, inc=1, device_id={"section": sec(i)}, device_id_type=MESH)
    for j in range(1, MP):
        pl.semaphore_signal(barrier, inc=1, device_id={"mp": core(j)}, device_id_type=MESH)

    def norm_into(G, values, gain):
        inverse = lax.rsqrt(jnp.mean(values * values, axis=-1, keepdims=True) + epsilon)
        n = (values * inverse * gain).astype(bf16)
        for c in range(CHUNKS):
            G[c, me, mm] = n[:, c * KC : (c + 1) * KC]

    def gather_start(G, ss, rs):
        for c in range(CHUNKS):
            own = G.at[c, me, mm]
            for i in range(1, S):
                send(own, own, ss.at[c, i - 1], rs.at[c, i - 1], section=sec(i))
            for j in range(1, MP):
                k = S - 1 + (j - 1) * S
                send(own, own, ss.at[c, k], rs.at[c, k], mp=core(j))

    def gather_pass(G, ss, rs, c):
        for i in range(1, S):
            got = G.at[c, sec(-i), mm]
            arrive(got, ss.at[c, i - 1], rs.at[c, i - 1], section=sec(i))
            for j in range(1, MP):
                k = S - 1 + (j - 1) * S + i
                send(got, got, ss.at[c, k], rs.at[c, k], mp=core(j))

    def gather_end(G, ss, rs, c):
        for j in range(1, MP):
            for i in range(S):
                k = S - 1 + (j - 1) * S + i
                got = G.at[c, sec(-i), core(-j)]
                arrive(got, ss.at[c, k], rs.at[c, k], mp=core(j))

    norm_into(G1, tokens[...].astype(f32), mix_gain[...].astype(f32).reshape(1, D))
    DB[me] = jnp.zeros(DB.shape[1:], f32)
    DB[me, 0:S, 0:heads] = decay[0, 0]
    pl.semaphore_wait(barrier, S - 1 + MP - 1)
    gather_start(G1, g1s, g1r)

    copies[3].wait()
    for q in range(S):
        STS[q] = SF[q].reshape(IW, SF.shape[-1]).astype(bf16)
    ST[me] = STS[me]
    for i in range(1, S):
        send(DB.at[me], DB.at[me], dbs.at[i - 1], dbr.at[i - 1], section=sec(i))
        send(STS.at[sec(i)], ST.at[me], sts.at[i - 1], str_.at[i - 1], section=sec(i))

    for k in (0, 1, 2):
        copies[k].wait()

    def project(G, ss, rs, W, side):
        wide, extra = W.shape[1], side.shape[0]
        gather_pass(G, ss, rs, 0)
        for c in range(CHUNKS):
            if c + 1 < CHUNKS:
                gather_pass(G, ss, rs, c + 1)
            gather_end(G, ss, rs, c)
            rowsets = G[c].reshape(T, KC)
            part = jnp.dot(rowsets, W[c * KC : (c + 1) * KC, :], preferred_element_type=f32)
            more = dot(rowsets, side[:, c * KC : (c + 1) * KC], 1, 1)
            if c == 0:
                acc[:, 0:wide] = part
                acc[:, wide : wide + extra] = more
            else:
                acc[:, 0:wide] += part
                acc[:, wide : wide + extra] += more

    acc[:, 2 * IW + GW :] = jnp.zeros((T, 128), f32)
    project(G1, g1s, g1r, W1, step_w)
    GP[me] = acc[:, 2 * IW : 2 * IW + GW].astype(bf16)
    for i in range(1, S):
        send(GP.at[me], GP.at[me], gps.at[i - 1], gpr.at[i - 1], section=sec(i))

    lane = lax.broadcasted_iota(jnp.int32, (1, 128), 1)
    wide = lax.broadcasted_iota(jnp.int32, (1, IW), 1) // HP

    def spread_scalars(ref, index):
        row = jnp.zeros(index.shape, f32)
        for h in range(heads):
            row = jnp.where(index == h, ref[h], row)
        return row

    def expand(cols):
        full = jnp.broadcast_to(cols[:, 0:1], (cols.shape[0], IW))
        for h in range(1, heads):
            full = jnp.where(wide == h, cols[:, h : h + 1], full)
        return full

    x = acc[:, 2 * IW + GW : 2 * IW + GW + 128] + spread_scalars(step_bias, lane)
    step = jnp.maximum(x, 0.0) + jnp.log1p(jnp.exp(-jnp.abs(x)))
    rates = -jnp.exp(spread_scalars(rate_log, lane))
    t_row = lax.broadcasted_iota(jnp.int32, (T, T), 0)
    t_col = lax.broadcasted_iota(jnp.int32, (T, T), 1)
    causal = t_row >= t_col
    log_decay = jnp.dot(
        causal.astype(f32), step * rates, preferred_element_type=f32, precision=lax.Precision.HIGHEST
    )
    ld_rows = log_decay.T
    st_rows = step.T
    inner = acc[:, 0:IW].astype(bf16)
    inner_f = inner.astype(f32)
    gates = acc[:, IW : 2 * IW]
    silu = gates / (1.0 + jnp.exp(-gates))
    skip = spread_scalars(skip_scale, wide) * inner_f
    reach = expand(jnp.exp(log_decay))

    for i in range(1, S):
        arrive(DB.at[sec(-i)], dbs.at[i - 1], dbr.at[i - 1], section=sec(i))
        arrive(ST.at[sec(-i)], sts.at[i - 1], str_.at[i - 1], section=sec(i))
    later = jnp.zeros((1, 128), f32)
    factors = [None] * S
    for c in reversed(range(S)):
        factors[c] = jnp.exp(later)
        later = later + DB[c, pl.ds(me, 1), :]
    for h in range(heads):
        total = factors[0][:, h : h + 1] * ST[0, h * HP : (h + 1) * HP, :].astype(f32)
        for c in range(1, S):
            total += factors[c][:, h : h + 1] * ST[c, h * HP : (h + 1) * HP, :].astype(f32)
        final_state[h] = total
    start = jnp.concatenate([final_state[h].astype(bf16) for h in range(heads)], axis=0)

    for i in range(1, S):
        arrive(GP.at[sec(-i)], gps.at[i - 1], gpr.at[i - 1], section=sec(i))
    writer = jnp.concatenate([GP[s] for s in range(S // 2)], axis=1)
    reader = jnp.concatenate([GP[s] for s in range(S // 2, S)], axis=1)
    affinity = dot(reader, writer, 1, 1)
    y = dot(reader, start, 1, 1) * reach + skip
    intra = jnp.zeros((T, IW), f32)
    for h in range(heads):
        gap = jnp.where(causal, log_decay[:, h : h + 1] - ld_rows[h : h + 1, :], 0.0)
        mixing = jnp.where(causal, affinity * jnp.exp(gap) * st_rows[h : h + 1, :], 0.0).astype(bf16)
        intra = jnp.where(wide == h, jnp.dot(mixing, inner, preferred_element_type=f32), intra)
    gated = (y + intra) * silu
    SQ[me] = dot(jnp.ones((8, IW), f32), gated * gated, 1, 1, precision=lax.Precision.HIGHEST)
    for i in range(1, S):
        send(SQ.at[me], SQ.at[me], sqs.at[i - 1], sqr.at[i - 1], section=sec(i))
    lhs = (gated * norm_gain[...].astype(f32).reshape(1, IW)).astype(bf16)

    def reduce_send(SND, ss, rs, c, value):
        value = value.astype(bf16).reshape(S, MP, rows, KC)
        for s in range(S):
            for m in range(MP):
                SND[c, m, s] = value[s, m]

    def scatter_pairs(SND, RCV, ss, rs, c):
        for j in range(1, MP):
            send(SND.at[c, core(j)], RCV.at[c, j - 1], ss.at[c, j - 1], rs.at[c, j - 1], mp=core(j))

    def scatter_sections(SND, RCV, ss, rs, MID, RCM, ms, mr, c):
        for j in range(1, MP):
            arrive(RCV.at[c, j - 1], ss.at[c, j - 1], rs.at[c, j - 1], mp=core(j))
        total = SND[c, mm].astype(f32)
        for j in range(1, MP):
            total += RCV[c, j - 1].astype(f32)
        MID[c] = total.astype(bf16)
        for i in range(1, S):
            send(MID.at[c, sec(i)], RCM.at[c, i - 1], ms.at[c, i - 1], mr.at[c, i - 1], section=sec(i))

    def scatter_end(MID, RCM, ms, mr, c):
        total = MID[c, me].astype(f32)
        for i in range(1, S):
            arrive(RCM.at[c, i - 1], ms.at[c, i - 1], mr.at[c, i - 1], section=sec(i))
            total += RCM[c, i - 1].astype(f32)
        return total

    copies[4].wait()
    inverse = None
    for c in range(CHUNKS):
        value = jnp.dot(lhs, Wo[:, c * KC : (c + 1) * KC], preferred_element_type=f32)
        if inverse is None:
            squares = SQ[me]
            for i in range(1, S):
                arrive(SQ.at[sec(-i)], sqs.at[i - 1], sqr.at[i - 1], section=sec(i))
                squares += SQ[sec(-i)]
            inverse = lax.rsqrt(squares / (S * IW) + epsilon)
            inverse = jnp.broadcast_to(inverse[0:1, :], (128, T)).T[:, 0:1]
        reduce_send(SND1, r1s, r1r, c, value * inverse)
        scatter_pairs(SND1, RCV1, r1s, r1r, c)
        if c:
            scatter_sections(SND1, RCV1, r1s, r1r, MID1, RCM1, m1s, m1r, c - 1)
    scatter_sections(SND1, RCV1, r1s, r1r, MID1, RCM1, m1s, m1r, CHUNKS - 1)

    tail = jnp.exp(log_decay[T - 1 : T, :] - log_decay) * step
    added = dot((inner_f * expand(tail)).astype(bf16), writer, 0, 0)
    last = jnp.exp(log_decay[T - 1 : T, :])
    for h in range(heads):
        final_state[h] = last[:, h : h + 1] * final_state[h] + added[h * HP : (h + 1) * HP, :]

    for c in range(CHUNKS):
        cols = slice(c * KC, (c + 1) * KC)
        RES[:, cols] = (
            tokens[:, cols].astype(f32) + scatter_end(MID1, RCM1, m1s, m1r, c)
        ).astype(bf16)
    norm_into(G2, RES[...].astype(f32), att_gain[...].astype(f32).reshape(1, D))
    gather_start(G2, g2s, g2r)
    for k in (5, 6, 7):
        copies[k].wait()
    acc[:, HD : 2 * HD] = jnp.zeros((T, HD), f32)
    project(G2, g2s, g2r, W2, WKV)
    QB[me] = acc[:, 0:HD].astype(bf16)
    for i in range(1, S):
        send(QB.at[me], QB.at[me], qbs.at[i - 1], qbr.at[i - 1], section=sec(i))
    KVB[me] = acc[:, HD : 2 * HD].astype(bf16)
    for i in range(1, S):
        send(KVB.at[me], KVB.at[me], kvs.at[i - 1], kvr.at[i - 1], section=sec(i))

    scale = 1.0 / math.sqrt(HD)
    held = CK.shape[0]
    position = lax.broadcasted_iota(jnp.int32, (held, 1), 0) + me * held
    bias = jnp.where(position >= held * S - doc_offset[0], 0.0, masked_low).astype(f32)

    def attend(q, keys, values, low):
        logits = dot(keys, q, 1, 1) + low
        top = jnp.max(logits, axis=0, keepdims=True)
        weights = jnp.exp((logits - top) * scale)
        total = jnp.sum(weights, axis=0, keepdims=True)
        out = dot(values, weights.astype(bf16), 0, 0)
        return top * scale, total, out

    def cached(q):
        return attend(q, CK[:, 0:HD], CK[:, HD : 2 * HD], bias)

    for i in range(1, S):
        slot = sec(-i)
        arrive(QB.at[slot], qbs.at[i - 1], qbr.at[i - 1], section=sec(i))
        top, total, out = cached(QB[slot])
        ACS[i - 1] = (out / total).astype(bf16)
        LS[i - 1, 0:8] = jnp.broadcast_to(top, (8, T))
        LS[i - 1, 8:16] = jnp.broadcast_to(total, (8, T))
        send(LS.at[i - 1], LR.at[i - 1], lss.at[i - 1], lsr.at[i - 1], section=slot)
        send(ACS.at[i - 1], ACR.at[i - 1], acs.at[i - 1], acr.at[i - 1], section=slot)
    parts = [cached(QB[me])]
    for i in range(1, S):
        arrive(KVB.at[sec(-i)], kvs.at[i - 1], kvr.at[i - 1], section=sec(i))
    pieces = jnp.concatenate([KVB[s][:, 0:KW].astype(f32) for s in range(S)], axis=1).astype(bf16)
    window_kv[...] = pieces
    new_low = jnp.where(t_row <= t_col, 0.0, masked_low).astype(f32)
    parts.append(attend(QB[me], pieces[:, 0:HD], pieces[:, HD : 2 * HD], new_low))
    copies[8].wait()
    top = jnp.maximum(parts[0][0], parts[1][0])
    for i in range(1, S):
        arrive(LR.at[i - 1], lss.at[i - 1], lsr.at[i - 1], section=sec(i))
        top = jnp.maximum(top, LR[i - 1, 0:1, :])
    total = jnp.zeros((1, T), f32)
    context = jnp.zeros((HD, T), f32)
    for p in parts:
        weight = jnp.exp(p[0] - top)
        total += weight * p[1]
        context += weight * p[2]
    for i in range(1, S):
        weight = jnp.exp(LR[i - 1, 0:1, :] - top) * LR[i - 1, 8:9, :]
        total += weight
        arrive(ACR.at[i - 1], acs.at[i - 1], acr.at[i - 1], section=sec(i))
        context += weight * ACR[i - 1].astype(f32)
    context = (context / total).T.astype(bf16)

    for c in range(CHUNKS):
        value = jnp.dot(context, Wc[:, c * KC : (c + 1) * KC], preferred_element_type=f32)
        reduce_send(SND2, r2s, r2r, c, value)
        scatter_pairs(SND2, RCV2, r2s, r2r, c)
        if c:
            scatter_sections(SND2, RCV2, r2s, r2r, MID2, RCM2, m2s, m2r, c - 1)
    scatter_sections(SND2, RCV2, r2s, r2r, MID2, RCM2, m2s, m2r, CHUNKS - 1)
    for c in range(CHUNKS):
        cols = slice(c * KC, (c + 1) * KC)
        hidden[:, cols] = (
            RES[:, cols].astype(f32) + scatter_end(MID2, RCM2, m2s, m2r, c)
        ).astype(bf16)
    for d in sent:
        d.wait_send()


def copy_kernel(a, b, c, x, y, z, i, j, k, sem):
    trips = ((a, i, x), (b, j, y), (c, k, z))
    loads = [pltpu.make_async_copy(src, mid, sem.at[n]) for n, (src, mid, _) in enumerate(trips)]
    stores = [pltpu.make_async_copy(mid, dst, sem.at[n + 3]) for n, (_, mid, dst) in enumerate(trips)]
    for d in loads:
        d.start()
    for d, e in zip(loads, stores):
        d.wait()
        e.start()
    for e in stores:
        e.wait()


def local(
    S, MP,
    tokens, mix_gain, inner_w, gate_w, group_w, step_w, step_bias, rate_log, skip_scale, norm_gain,
    out_w, states, decay, att_gain, query_w, keyval_w, context_w, cache, doc_offset,
):
    rows, D = tokens.shape
    T = rows * S * MP
    KC = D // CHUNKS
    IW = inner_w.shape[1]
    GW = group_w.shape[1]
    heads = step_w.shape[1]
    HP = IW // heads
    NS = states.shape[-1]
    HD = query_w.shape[1]
    dma = pltpu.SemaphoreType.DMA
    vmem = pltpu.VMEM

    def both(*shape):
        return [dma(shape), dma(shape)]

    def scatter():
        return [
            vmem((CHUNKS, MP, S, rows, KC), bf16), vmem((CHUNKS, MP - 1, S, rows, KC), bf16),
            *both(CHUNKS, MP - 1),
            vmem((CHUNKS, S, rows, KC), bf16), vmem((CHUNKS, S - 1, rows, KC), bf16),
            *both(CHUNKS, S - 1),
        ]

    hops = S - 1 + (MP - 1) * S
    scratch = [
        vmem((D, 2 * IW + GW), bf16), vmem(out_w.shape, bf16),
        vmem((D, HD), bf16), vmem(keyval_w.shape[::-1], bf16), vmem(context_w.shape, bf16),
        vmem((cache.shape[0], 2 * HD), bf16), vmem(states.shape[2:], f32), dma((9,)),
        vmem((CHUNKS, S, MP, rows, KC), bf16), vmem((CHUNKS, S, MP, rows, KC), bf16),
        *both(CHUNKS, hops), *both(CHUNKS, hops),
        vmem((T, 2 * IW + GW + 128), f32),
        vmem((S, T, GW), bf16), *both(S - 1),
        vmem((S, IW, NS), bf16), vmem((S, IW, NS), bf16), *both(S - 1),
        vmem((S, 8, 128), f32), *both(S - 1),
        vmem((S, 8, T), f32), *both(S - 1),
        *scatter(), *scatter(),
        vmem((rows, D), bf16),
        vmem((S, T, HD), bf16), *both(S - 1),
        vmem((S, T, HD), bf16), *both(S - 1),
        vmem((S - 1, HD, T), bf16), vmem((S - 1, HD, T), bf16), *both(S - 1),
        vmem((S - 1, 16, T), f32), vmem((S - 1, 16, T), f32), *both(S - 1),
    ]
    v = pl.BlockSpec(memory_space=pltpu.VMEM)
    a = pl.BlockSpec(memory_space=pl.ANY)
    s = pl.BlockSpec(memory_space=pltpu.SMEM)
    hidden, final_state, window_kv = pl.pallas_call(
        functools.partial(kernel, S, MP),
        out_shape=(
            jax.ShapeDtypeStruct((rows, D), bf16),
            jax.ShapeDtypeStruct((heads, HP, NS), f32),
            jax.ShapeDtypeStruct((T, 2 * HD), bf16),
        ),
        in_specs=[v, v, a, a, a, v, s, s, s, v, a, a, v, v, a, a, a, a, s],
        out_specs=(v, v, v),
        scratch_shapes=scratch,
        compiler_params=pltpu.CompilerParams(
            collective_id=0, has_side_effects=True, vmem_limit_bytes=60 * 1024 * 1024
        ),
    )(
        tokens, mix_gain, inner_w, gate_w, group_w, step_w.T, step_bias, rate_log,
        skip_scale, norm_gain, out_w, states, decay, att_gain,
        query_w, keyval_w.T, context_w, cache.reshape(cache.shape[0], 2 * HD), doc_offset,
    )
    results = (hidden, final_state, window_kv)
    hidden, final_state, window_kv = pl.pallas_call(
        copy_kernel,
        out_shape=tuple(jax.ShapeDtypeStruct(x.shape, x.dtype) for x in results),
        in_specs=[a, a, a],
        out_specs=(a, a, a),
        scratch_shapes=[*(vmem(x.shape, x.dtype) for x in results), dma((6,))],
    )(*results)
    return hidden, final_state, window_kv[:, None, :]


def solution(mesh):
    S, MP = mesh.shape["section"], mesh.shape["mp"]
    both = ("section", "mp")
    in_specs = (
        P(("dp", "section", "mp"), None),
        P(),
        P(None, both),
        P(None, both),
        P(None, both),
        P(None, both),
        P(both),
        P(both),
        P(both),
        P(both),
        P(both, None),
        P(("dp", "section"), "mp", None, None, None, None),
        P(("dp", "section"), "mp", None, None),
        P(),
        P(None, both),
        P(None, both),
        P(both, None),
        P(("dp", "section"), "mp", None),
        P("dp"),
    )
    out_specs = (
        P(("dp", "section", "mp"), None),
        P(("dp", "section", "mp"), None, None),
        P("dp", "mp", None),
    )
    return jax.shard_map(
        functools.partial(local, S, MP), mesh=mesh, in_specs=in_specs, out_specs=out_specs, check_vma=False
    )
```

```python
import functools
import math

import jax
import jax.numpy as jnp
from jax import lax
from jax.experimental import pallas as pl
from jax.experimental.pallas import tpu as pltpu
from jax.sharding import PartitionSpec as P

epsilon = 1e-05
masked_low = -1e30
MESH = pl.DeviceIdType.MESH
f32 = jnp.float32
bf16 = jnp.bfloat16
CHUNKS = 2


def dot(a, b, ca, cb, **kw):
    return lax.dot_general(a, b, (((ca,), (cb,)), ((), ())), preferred_element_type=f32, **kw)


def kernel(
    S, MP,
    tokens, mix_gain, inner_w, gate_w, group_w, step_w, step_bias, rate_log, skip_scale, norm_gain,
    out_w, states, decay, att_gain, query_w, keyval_w, context_w, cache, doc_offset,
    hidden, final_state, window_kv,
    W1, Wo, W2, WKV, Wc, CK, SF, load_sem,
    G1, G2, g1s, g1r, g2s, g2r,
    acc, GP, gps, gpr, STS, ST, sts, str_, DB, dbs, dbr, SQ, sqs, sqr,
    SND1, RCV1, r1s, r1r, MID1, RCM1, m1s, m1r,
    SND2, RCV2, r2s, r2r, MID2, RCM2, m2s, m2r,
    RES, QB, qbs, qbr, KVB, kvs, kvr, ACS, ACR, acs, acr, LS, LR, lss, lsr,
):
    me = lax.axis_index("section")
    mm = lax.axis_index("mp")
    rows, D = tokens.shape
    T = rows * S * MP
    KC = D // CHUNKS
    IW = inner_w.shape[1]
    GW = group_w.shape[1]
    heads = step_w.shape[0]
    HP = IW // heads
    HD = query_w.shape[1]
    KW = keyval_w.shape[0]
    sent = []

    def sec(i):
        return lax.rem(me + i + S, S)

    def core(j):
        return lax.rem(mm + j + MP, MP)

    def rcopy(src, dst, ss, rs, **where):
        return pltpu.make_async_remote_copy(
            src_ref=src, dst_ref=dst, send_sem=ss, recv_sem=rs, device_id=where, device_id_type=MESH
        )

    def send(src, dst, ss, rs, **where):
        d = rcopy(src, dst, ss, rs, **where)
        d.start()
        sent.append(d)

    def arrive(dst, ss, rs, **where):
        rcopy(dst, dst, ss, rs, **where).wait_recv()

    loads = [
        (inner_w, W1.at[:, 0:IW]),
        (gate_w, W1.at[:, IW : 2 * IW]),
        (group_w, W1.at[:, 2 * IW : 2 * IW + GW]),
        (states.at[0, 0], SF),
        (out_w, Wo),
        (query_w, W2),
        (keyval_w, WKV),
        (cache, CK),
        (context_w, Wc),
    ]
    copies = [pltpu.make_async_copy(a, b, load_sem.at[k]) for k, (a, b) in enumerate(loads)]
    for c in copies:
        c.start()

    barrier = pltpu.get_barrier_semaphore()
    for i in range(1, S):
        pl.semaphore_signal(barrier, inc=1, device_id={"section": sec(i)}, device_id_type=MESH)
    for j in range(1, MP):
        pl.semaphore_signal(barrier, inc=1, device_id={"mp": core(j)}, device_id_type=MESH)

    def norm_into(G, values, gain):
        inverse = lax.rsqrt(jnp.mean(values * values, axis=-1, keepdims=True) + epsilon)
        n = (values * inverse * gain).astype(bf16)
        for c in range(CHUNKS):
            G[c, me, mm] = n[:, c * KC : (c + 1) * KC]

    def gather_start(G, ss, rs):
        for c in range(CHUNKS):
            own = G.at[c, me, mm]
            for i in range(1, S):
                send(own, own, ss.at[c, i - 1], rs.at[c, i - 1], section=sec(i))
            for j in range(1, MP):
                k = S - 1 + (j - 1) * S
                send(own, own, ss.at[c, k], rs.at[c, k], mp=core(j))

    def gather_pass(G, ss, rs, c):
        for i in range(1, S):
            got = G.at[c, sec(-i), mm]
            arrive(got, ss.at[c, i - 1], rs.at[c, i - 1], section=sec(i))
            for j in range(1, MP):
                k = S - 1 + (j - 1) * S + i
                send(got, got, ss.at[c, k], rs.at[c, k], mp=core(j))

    def gather_end(G, ss, rs, c):
        for j in range(1, MP):
            for i in range(S):
                k = S - 1 + (j - 1) * S + i
                got = G.at[c, sec(-i), core(-j)]
                arrive(got, ss.at[c, k], rs.at[c, k], mp=core(j))

    norm_into(G1, tokens[...].astype(f32), mix_gain[...].astype(f32).reshape(1, D))
    DB[me] = jnp.zeros(DB.shape[1:], f32)
    DB[me, 0:S, 0:heads] = decay[0, 0]
    pl.semaphore_wait(barrier, S - 1 + MP - 1)
    gather_start(G1, g1s, g1r)

    copies[3].wait()
    for q in range(S):
        STS[q] = SF[q].reshape(IW, SF.shape[-1]).astype(bf16)
    ST[me] = STS[me]
    for i in range(1, S):
        send(DB.at[me], DB.at[me], dbs.at[i - 1], dbr.at[i - 1], section=sec(i))
        send(STS.at[sec(i)], ST.at[me], sts.at[i - 1], str_.at[i - 1], section=sec(i))

    for k in (0, 1, 2):
        copies[k].wait()

    def project(G, ss, rs, W, side):
        wide, extra = W.shape[1], side.shape[0]
        gather_pass(G, ss, rs, 0)
        for c in range(CHUNKS):
            if c + 1 < CHUNKS:
                gather_pass(G, ss, rs, c + 1)
            gather_end(G, ss, rs, c)
            rowsets = G[c].reshape(T, KC)
            part = jnp.dot(rowsets, W[c * KC : (c + 1) * KC, :], preferred_element_type=f32)
            more = dot(rowsets, side[:, c * KC : (c + 1) * KC], 1, 1)
            if c == 0:
                acc[:, 0:wide] = part
                acc[:, wide : wide + extra] = more
            else:
                acc[:, 0:wide] += part
                acc[:, wide : wide + extra] += more

    acc[:, 2 * IW + GW :] = jnp.zeros((T, 128), f32)
    project(G1, g1s, g1r, W1, step_w)
    GP[me] = acc[:, 2 * IW : 2 * IW + GW].astype(bf16)
    for i in range(1, S):
        send(GP.at[me], GP.at[me], gps.at[i - 1], gpr.at[i - 1], section=sec(i))

    lane = lax.broadcasted_iota(jnp.int32, (1, 128), 1)
    wide = lax.broadcasted_iota(jnp.int32, (1, IW), 1) // HP

    def spread_scalars(ref, index):
        row = jnp.zeros(index.shape, f32)
        for h in range(heads):
            row = jnp.where(index == h, ref[h], row)
        return row

    def expand(cols):
        full = jnp.broadcast_to(cols[:, 0:1], (cols.shape[0], IW))
        for h in range(1, heads):
            full = jnp.where(wide == h, cols[:, h : h + 1], full)
        return full

    x = acc[:, 2 * IW + GW : 2 * IW + GW + 128] + spread_scalars(step_bias, lane)
    step = jnp.maximum(x, 0.0) + jnp.log1p(jnp.exp(-jnp.abs(x)))
    rates = -jnp.exp(spread_scalars(rate_log, lane))
    t_row = lax.broadcasted_iota(jnp.int32, (T, T), 0)
    t_col = lax.broadcasted_iota(jnp.int32, (T, T), 1)
    causal = t_row >= t_col
    log_decay = jnp.dot(
        causal.astype(f32), step * rates, preferred_element_type=f32, precision=lax.Precision.HIGHEST
    )
    ld_rows = log_decay.T
    st_rows = step.T
    inner = acc[:, 0:IW].astype(bf16)
    inner_f = inner.astype(f32)
    gates = acc[:, IW : 2 * IW]
    silu = gates / (1.0 + jnp.exp(-gates))
    skip = spread_scalars(skip_scale, wide) * inner_f
    reach = expand(jnp.exp(log_decay))

    for i in range(1, S):
        arrive(DB.at[sec(-i)], dbs.at[i - 1], dbr.at[i - 1], section=sec(i))
        arrive(ST.at[sec(-i)], sts.at[i - 1], str_.at[i - 1], section=sec(i))
    later = jnp.zeros((1, 128), f32)
    factors = [None] * S
    for c in reversed(range(S)):
        factors[c] = jnp.exp(later)
        later = later + DB[c, pl.ds(me, 1), :]
    for h in range(heads):
        total = factors[0][:, h : h + 1] * ST[0, h * HP : (h + 1) * HP, :].astype(f32)
        for c in range(1, S):
            total += factors[c][:, h : h + 1] * ST[c, h * HP : (h + 1) * HP, :].astype(f32)
        final_state[h] = total
    start = jnp.concatenate([final_state[h].astype(bf16) for h in range(heads)], axis=0)

    for i in range(1, S):
        arrive(GP.at[sec(-i)], gps.at[i - 1], gpr.at[i - 1], section=sec(i))
    writer = jnp.concatenate([GP[s] for s in range(S // 2)], axis=1)
    reader = jnp.concatenate([GP[s] for s in range(S // 2, S)], axis=1)
    affinity = dot(reader, writer, 1, 1)
    y = dot(reader, start, 1, 1) * reach + skip
    intra = jnp.zeros((T, IW), f32)
    for h in range(heads):
        gap = jnp.where(causal, log_decay[:, h : h + 1] - ld_rows[h : h + 1, :], 0.0)
        mixing = jnp.where(causal, affinity * jnp.exp(gap) * st_rows[h : h + 1, :], 0.0).astype(bf16)
        intra = jnp.where(wide == h, jnp.dot(mixing, inner, preferred_element_type=f32), intra)
    gated = (y + intra) * silu
    SQ[me] = dot(jnp.ones((8, IW), f32), gated * gated, 1, 1, precision=lax.Precision.HIGHEST)
    for i in range(1, S):
        send(SQ.at[me], SQ.at[me], sqs.at[i - 1], sqr.at[i - 1], section=sec(i))
    lhs = (gated * norm_gain[...].astype(f32).reshape(1, IW)).astype(bf16)

    def reduce_send(SND, ss, rs, c, value):
        value = value.astype(bf16).reshape(S, MP, rows, KC)
        for s in range(S):
            for m in range(MP):
                SND[c, m, s] = value[s, m]

    def scatter_pairs(SND, RCV, ss, rs, c):
        for j in range(1, MP):
            send(SND.at[c, core(j)], RCV.at[c, j - 1], ss.at[c, j - 1], rs.at[c, j - 1], mp=core(j))

    def scatter_sections(SND, RCV, ss, rs, MID, RCM, ms, mr, c):
        for j in range(1, MP):
            arrive(RCV.at[c, j - 1], ss.at[c, j - 1], rs.at[c, j - 1], mp=core(j))
        total = SND[c, mm].astype(f32)
        for j in range(1, MP):
            total += RCV[c, j - 1].astype(f32)
        MID[c] = total.astype(bf16)
        for i in range(1, S):
            send(MID.at[c, sec(i)], RCM.at[c, i - 1], ms.at[c, i - 1], mr.at[c, i - 1], section=sec(i))

    def scatter_end(MID, RCM, ms, mr, c):
        total = MID[c, me].astype(f32)
        for i in range(1, S):
            arrive(RCM.at[c, i - 1], ms.at[c, i - 1], mr.at[c, i - 1], section=sec(i))
            total += RCM[c, i - 1].astype(f32)
        return total

    copies[4].wait()
    inverse = None
    for c in range(CHUNKS):
        value = jnp.dot(lhs, Wo[:, c * KC : (c + 1) * KC], preferred_element_type=f32)
        if inverse is None:
            squares = SQ[me]
            for i in range(1, S):
                arrive(SQ.at[sec(-i)], sqs.at[i - 1], sqr.at[i - 1], section=sec(i))
                squares += SQ[sec(-i)]
            inverse = lax.rsqrt(squares / (S * IW) + epsilon)
            inverse = jnp.broadcast_to(inverse[0:1, :], (128, T)).T[:, 0:1]
        reduce_send(SND1, r1s, r1r, c, value * inverse)
        scatter_pairs(SND1, RCV1, r1s, r1r, c)
        if c:
            scatter_sections(SND1, RCV1, r1s, r1r, MID1, RCM1, m1s, m1r, c - 1)
    scatter_sections(SND1, RCV1, r1s, r1r, MID1, RCM1, m1s, m1r, CHUNKS - 1)

    tail = jnp.exp(log_decay[T - 1 : T, :] - log_decay) * step
    added = dot((inner_f * expand(tail)).astype(bf16), writer, 0, 0)
    last = jnp.exp(log_decay[T - 1 : T, :])
    for h in range(heads):
        final_state[h] = last[:, h : h + 1] * final_state[h] + added[h * HP : (h + 1) * HP, :]

    for c in range(CHUNKS):
        cols = slice(c * KC, (c + 1) * KC)
        RES[:, cols] = (
            tokens[:, cols].astype(f32) + scatter_end(MID1, RCM1, m1s, m1r, c)
        ).astype(bf16)
    norm_into(G2, RES[...].astype(f32), att_gain[...].astype(f32).reshape(1, D))
    gather_start(G2, g2s, g2r)
    for k in (5, 6, 7):
        copies[k].wait()
    acc[:, HD : 2 * HD] = jnp.zeros((T, HD), f32)
    project(G2, g2s, g2r, W2, WKV)
    QB[me] = acc[:, 0:HD].astype(bf16)
    for i in range(1, S):
        send(QB.at[me], QB.at[me], qbs.at[i - 1], qbr.at[i - 1], section=sec(i))
    KVB[me] = acc[:, HD : 2 * HD].astype(bf16)
    for i in range(1, S):
        send(KVB.at[me], KVB.at[me], kvs.at[i - 1], kvr.at[i - 1], section=sec(i))

    scale = 1.0 / math.sqrt(HD)
    held = CK.shape[0]
    position = lax.broadcasted_iota(jnp.int32, (held, 1), 0) + me * held
    bias = jnp.where(position >= held * S - doc_offset[0], 0.0, masked_low).astype(f32)

    def attend(q, keys, values, low):
        logits = dot(keys, q, 1, 1) + low
        top = jnp.max(logits, axis=0, keepdims=True)
        weights = jnp.exp((logits - top) * scale)
        total = jnp.sum(weights, axis=0, keepdims=True)
        out = dot(values, weights.astype(bf16), 0, 0)
        return top * scale, total, out

    def cached(q):
        return attend(q, CK[:, 0:HD], CK[:, HD : 2 * HD], bias)

    for i in range(1, S):
        slot = sec(-i)
        arrive(QB.at[slot], qbs.at[i - 1], qbr.at[i - 1], section=sec(i))
        top, total, out = cached(QB[slot])
        ACS[i - 1] = (out / total).astype(bf16)
        LS[i - 1, 0:8] = jnp.broadcast_to(top, (8, T))
        LS[i - 1, 8:16] = jnp.broadcast_to(total, (8, T))
        send(LS.at[i - 1], LR.at[i - 1], lss.at[i - 1], lsr.at[i - 1], section=slot)
        send(ACS.at[i - 1], ACR.at[i - 1], acs.at[i - 1], acr.at[i - 1], section=slot)
    parts = [cached(QB[me])]
    for i in range(1, S):
        arrive(KVB.at[sec(-i)], kvs.at[i - 1], kvr.at[i - 1], section=sec(i))
    pieces = jnp.concatenate([KVB[s][:, 0:KW].astype(f32) for s in range(S)], axis=1).astype(bf16)
    window_kv[...] = pieces
    new_low = jnp.where(t_row <= t_col, 0.0, masked_low).astype(f32)
    parts.append(attend(QB[me], pieces[:, 0:HD], pieces[:, HD : 2 * HD], new_low))
    copies[8].wait()
    top = jnp.maximum(parts[0][0], parts[1][0])
    for i in range(1, S):
        arrive(LR.at[i - 1], lss.at[i - 1], lsr.at[i - 1], section=sec(i))
        top = jnp.maximum(top, LR[i - 1, 0:1, :])
    total = jnp.zeros((1, T), f32)
    context = jnp.zeros((HD, T), f32)
    for p in parts:
        weight = jnp.exp(p[0] - top)
        total += weight * p[1]
        context += weight * p[2]
    for i in range(1, S):
        weight = jnp.exp(LR[i - 1, 0:1, :] - top) * LR[i - 1, 8:9, :]
        total += weight
        arrive(ACR.at[i - 1], acs.at[i - 1], acr.at[i - 1], section=sec(i))
        context += weight * ACR[i - 1].astype(f32)
    context = (context / total).T.astype(bf16)

    for c in range(CHUNKS):
        value = jnp.dot(context, Wc[:, c * KC : (c + 1) * KC], preferred_element_type=f32)
        reduce_send(SND2, r2s, r2r, c, value)
        scatter_pairs(SND2, RCV2, r2s, r2r, c)
        if c:
            scatter_sections(SND2, RCV2, r2s, r2r, MID2, RCM2, m2s, m2r, c - 1)
    scatter_sections(SND2, RCV2, r2s, r2r, MID2, RCM2, m2s, m2r, CHUNKS - 1)
    for c in range(CHUNKS):
        cols = slice(c * KC, (c + 1) * KC)
        hidden[:, cols] = (
            RES[:, cols].astype(f32) + scatter_end(MID2, RCM2, m2s, m2r, c)
        ).astype(bf16)
    for d in sent:
        d.wait_send()


def copy_kernel(a, b, c, x, y, z, i, j, k, sem):
    trips = ((a, i, x), (b, j, y), (c, k, z))
    loads = [pltpu.make_async_copy(src, mid, sem.at[n]) for n, (src, mid, _) in enumerate(trips)]
    stores = [pltpu.make_async_copy(mid, dst, sem.at[n + 3]) for n, (_, mid, dst) in enumerate(trips)]
    for d in loads:
        d.start()
    for d, e in zip(loads, stores):
        d.wait()
        e.start()
    for e in stores:
        e.wait()


def local(
    S, MP,
    tokens, mix_gain, inner_w, gate_w, group_w, step_w, step_bias, rate_log, skip_scale, norm_gain,
    out_w, states, decay, att_gain, query_w, keyval_w, context_w, cache, doc_offset,
):
    rows, D = tokens.shape
    T = rows * S * MP
    KC = D // CHUNKS
    IW = inner_w.shape[1]
    GW = group_w.shape[1]
    heads = step_w.shape[1]
    HP = IW // heads
    NS = states.shape[-1]
    HD = query_w.shape[1]
    dma = pltpu.SemaphoreType.DMA
    vmem = pltpu.VMEM

    def both(*shape):
        return [dma(shape), dma(shape)]

    def scatter():
        return [
            vmem((CHUNKS, MP, S, rows, KC), bf16), vmem((CHUNKS, MP - 1, S, rows, KC), bf16),
            *both(CHUNKS, MP - 1),
            vmem((CHUNKS, S, rows, KC), bf16), vmem((CHUNKS, S - 1, rows, KC), bf16),
            *both(CHUNKS, S - 1),
        ]

    hops = S - 1 + (MP - 1) * S
    scratch = [
        vmem((D, 2 * IW + GW), bf16), vmem(out_w.shape, bf16),
        vmem((D, HD), bf16), vmem(keyval_w.shape[::-1], bf16), vmem(context_w.shape, bf16),
        vmem((cache.shape[0], 2 * HD), bf16), vmem(states.shape[2:], f32), dma((9,)),
        vmem((CHUNKS, S, MP, rows, KC), bf16), vmem((CHUNKS, S, MP, rows, KC), bf16),
        *both(CHUNKS, hops), *both(CHUNKS, hops),
        vmem((T, 2 * IW + GW + 128), f32),
        vmem((S, T, GW), bf16), *both(S - 1),
        vmem((S, IW, NS), bf16), vmem((S, IW, NS), bf16), *both(S - 1),
        vmem((S, 8, 128), f32), *both(S - 1),
        vmem((S, 8, T), f32), *both(S - 1),
        *scatter(), *scatter(),
        vmem((rows, D), bf16),
        vmem((S, T, HD), bf16), *both(S - 1),
        vmem((S, T, HD), bf16), *both(S - 1),
        vmem((S - 1, HD, T), bf16), vmem((S - 1, HD, T), bf16), *both(S - 1),
        vmem((S - 1, 16, T), f32), vmem((S - 1, 16, T), f32), *both(S - 1),
    ]
    v = pl.BlockSpec(memory_space=pltpu.VMEM)
    a = pl.BlockSpec(memory_space=pl.ANY)
    s = pl.BlockSpec(memory_space=pltpu.SMEM)
    hidden, final_state, window_kv = pl.pallas_call(
        functools.partial(kernel, S, MP),
        out_shape=(
            jax.ShapeDtypeStruct((rows, D), bf16),
            jax.ShapeDtypeStruct((heads, HP, NS), f32),
            jax.ShapeDtypeStruct((T, 2 * HD), bf16),
        ),
        in_specs=[v, v, a, a, a, v, s, s, s, v, a, a, v, v, a, a, a, a, s],
        out_specs=(v, v, v),
        scratch_shapes=scratch,
        compiler_params=pltpu.CompilerParams(
            collective_id=0, has_side_effects=True, vmem_limit_bytes=60 * 1024 * 1024
        ),
    )(
        tokens, mix_gain, inner_w, gate_w, group_w, step_w.T, step_bias, rate_log,
        skip_scale, norm_gain, out_w, states, decay, att_gain,
        query_w, keyval_w.T, context_w, cache.reshape(cache.shape[0], 2 * HD), doc_offset,
    )
    results = (hidden, final_state, window_kv)
    hidden, final_state, window_kv = pl.pallas_call(
        copy_kernel,
        out_shape=tuple(jax.ShapeDtypeStruct(x.shape, x.dtype) for x in results),
        in_specs=[a, a, a],
        out_specs=(a, a, a),
        scratch_shapes=[*(vmem(x.shape, x.dtype) for x in results), dma((6,))],
    )(*results)
    return hidden, final_state, window_kv[:, None, :]


def solution(mesh):
    S, MP = mesh.shape["section"], mesh.shape["mp"]
    both = ("section", "mp")
    in_specs = (
        P(("dp", "section", "mp"), None),
        P(),
        P(None, both),
        P(None, both),
        P(None, both),
        P(None, both),
        P(both),
        P(both),
        P(both),
        P(both),
        P(both, None),
        P(("dp", "section"), "mp", None, None, None, None),
        P(("dp", "section"), "mp", None, None),
        P(),
        P(None, both),
        P(None, both),
        P(both, None),
        P(("dp", "section"), "mp", None),
        P("dp"),
    )
    out_specs = (
        P(("dp", "section", "mp"), None),
        P(("dp", "section", "mp"), None, None),
        P("dp", "mp", None),
    )
    return jax.shard_map(
        functools.partial(local, S, MP), mesh=mesh, in_specs=in_specs, out_specs=out_specs, check_vma=False
    )
```
